128 devices in a mesh: video: 4 (over z), frame: 32 (over y, x, core).
Axes of the slice: x: 4, y: 4, z: 4, core: 2. Of those that a mesh axis runs over, the one named last changes fastest.
Arguments:
- patches: bfloat16 [4, 46656, 1152], P('video', 'frame'), may hold values from -6 to 6
- latents: bfloat16 [4, 64, 1152], P('video'), may hold values from -600 to 600
- gain: bfloat16 [1152], replicated, may hold values from 0.25 to 1.75
- w_query: bfloat16 [1152, 1152], replicated, may hold values from -0.1875 to 0.1875
- w_key: bfloat16 [1152, 1152], replicated, may hold values from -0.1875 to 0.1875
- w_value: bfloat16 [1152, 1152], replicated, may hold values from -0.1875 to 0.1875
- w_out: bfloat16 [1152, 1152], P(None, 'frame'), may hold values from -0.1875 to 0.1875
- cotangent: bfloat16 [4, 64, 1152], P('video', None, 'frame'), may hold values from -6 to 6
Outputs:
- attended: bfloat16 [4, 64, 1152], P('video', None, 'frame')
- patch_grad: bfloat16 [4, 46656, 1152], P('video', 'frame')
- kv_grad: float32 [1152, 2304], P(('video', 'frame'))
The draws below stay inside these ranges and needn't reach their ends.
All inputs are finite; a program needn't handle non-finite values.
Results may differ from the reference program's by a relative error of at most 0.04.
Values sent between devices are 32-bit elements; how exact they have to be, the bound alone decides.
No kernel may reach another device: no remote copies, remote signals or barrier semaphores. Data moves between devices by JAX's collectives and lax.ppermute only.
A program may use at most 192 MiB of HBM per device.

```python
import jax
import jax.numpy as jnp
from jax import lax

D = 1152
HEADS = 16
PATCHES = 729
NLAT = 64
FRAMES = 64
VIDEOS = 4
N_VIDEO = 4


def draw_latents(key, part):
    key = jax.random.fold_in(key, 11)
    base = jax.random.truncated_normal(key, -4.0, 4.0, (N_VIDEO, NLAT, D), jnp.float32)
    return (base * 3.0).astype(jnp.bfloat16)


def spiked(values, key, source, target, blocks, factor):
    owner, partner = [(jnp.arange(values.shape[position]) // (values.shape[position] // blocks)).reshape([-1 if axis == position else 1 for axis in range(values.ndim)]) for position in (source, target)]
    chosen = jax.random.permutation(key, blocks)[partner]
    strong = (owner == chosen) | (owner == (partner + blocks // 2) % blocks)
    return jnp.where(strong, factor * values, values)


def block_levels(own_key, extent, split, low, largest):
    level, own = 1.0, jax.random.fold_in(own_key, 6)
    for axis_at, blocks in split:
        draws = jnp.exp(jax.random.uniform(jax.random.fold_in(own, axis_at), (blocks,), jnp.float32, low / len(split), largest / len(split)))
        level = level * jnp.repeat(draws, extent[axis_at] // blocks).reshape([-1 if axis == axis_at else 1 for axis in range(len(extent))])
    return level


def bell_draw(own_key, shape, scale, reach, split=(), held_as=jnp.bfloat16):
    loudness = block_levels(own_key, shape, split, -0.22, 0.18) if split else 1.0
    drawn = jax.random.normal(own_key, shape, jnp.float32) * scale * loudness
    return jnp.minimum(jnp.maximum(drawn, -reach), reach).astype(held_as)


def bell_draw_with(own_key, extent, scale, limit, cuts, heavy, kind=jnp.bfloat16):
    drawn = scale * jax.random.normal(own_key, extent, jnp.float32)
    if cuts:
        drawn = drawn * block_levels(own_key, extent, cuts, -0.22, 0.18)
    return jnp.clip(spiked(drawn, jax.random.fold_in(own_key, 3), *heavy), -limit, limit).astype(kind)


def setup_inputs(seed: int = 0) -> dict:
    seeds = jax.random.split(jax.random.key(seed), 9)
    patches = bell_draw_with(seeds[0], (VIDEOS, FRAMES * PATCHES, D), 1.0, 6.0, ((0, 4), (1, 32)), (1, 2, 32, 2.75))
    latents = draw_latents(jax.random.fold_in(seeds[8], 71), 0)
    gain = jnp.clip(1.0 + 0.15 * jax.random.normal(seeds[2], (D,), jnp.float32), 0.25, 1.75).astype(jnp.bfloat16)
    w_query = bell_draw(seeds[3], (D, D), D ** -0.5, 0.1875)
    w_key = bell_draw(seeds[4], (D, D), D ** -0.5, 0.1875)
    w_value = bell_draw(seeds[5], (D, D), D ** -0.5, 0.1875)
    w_out = bell_draw(seeds[6], (D, D), D ** -0.5, 0.1875, ((1, 32),))
    cotangent = bell_draw(seeds[7], (VIDEOS, NLAT, D), 1.0, 6.0, ((0, 4), (2, 32)))
    return {"patches": patches, "latents": latents, "gain": gain, "w_query": w_query, "w_key": w_key, "w_value": w_value, "w_out": w_out, "cotangent": cotangent}


def layer_norm(values, gain):
    mean = lax.optimization_barrier(jnp.mean(values, axis=-1, keepdims=True))
    centred = values - mean
    var = lax.optimization_barrier(jnp.mean(centred * centred, axis=-1, keepdims=True))
    return centred * lax.rsqrt(var + 1e-06) * gain.astype(jnp.float32)

def one_video(frames, latent_rows, gain, w_query, w_key, w_value, w_out, cot_rows):
    rows = frames.shape[0]
    width = D // HEADS
    scale = 1.0 / width ** 0.5
    hp = lax.Precision.HIGHEST
    normed_f, norm_back = jax.vjp(lambda v: layer_norm(v, gain), frames.astype(jnp.float32))
    normed = normed_f.astype(jnp.bfloat16)
    keys = jnp.dot(normed, w_key, preferred_element_type=jnp.float32).astype(jnp.bfloat16)
    values = jnp.dot(normed, w_value, preferred_element_type=jnp.float32).astype(jnp.bfloat16)
    query = jnp.dot(latent_rows, w_query, preferred_element_type=jnp.float32).astype(jnp.bfloat16)
    qh = query.astype(jnp.float32).reshape(NLAT, HEADS, width)
    kh = keys.astype(jnp.float32).reshape(rows, HEADS, width)
    vh = values.astype(jnp.float32).reshape(rows, HEADS, width)
    scores = jnp.einsum('qhe,rhe->hqr', qh, kh, precision=hp) * scale
    top = lax.optimization_barrier(jnp.max(scores, axis=-1, keepdims=True))
    expo = jnp.exp(scores - top)
    total = lax.optimization_barrier(jnp.sum(expo, axis=-1, keepdims=True))
    probs = expo / total
    attn_h = jnp.einsum('hqr,rhe->qhe', probs, vh, precision=hp)
    attn = attn_h.reshape(NLAT, D)
    attended = jnp.dot(attn.astype(jnp.bfloat16), w_out, preferred_element_type=jnp.float32).astype(jnp.bfloat16)
    latent_cot = jnp.dot(cot_rows, w_out.T, preferred_element_type=jnp.float32)
    cot_h = latent_cot.reshape(NLAT, HEADS, width)
    drift = lax.optimization_barrier(jnp.sum(cot_h * attn_h, axis=-1)).T
    dprob = jnp.einsum('qhe,rhe->hqr', cot_h, vh, precision=hp)
    dscore = probs * (dprob - drift[:, :, None]) * scale
    key_cot = jnp.einsum('hqr,qhe->rhe', dscore, qh, precision=hp).reshape(rows, D).astype(jnp.bfloat16)
    value_cot = jnp.einsum('hqr,qhe->rhe', probs, cot_h, precision=hp).reshape(rows, D).astype(jnp.bfloat16)
    normed_cot = jnp.dot(key_cot, w_key.T, preferred_element_type=jnp.float32)
    normed_cot = normed_cot + jnp.dot(value_cot, w_value.T, preferred_element_type=jnp.float32)
    patch_grad = norm_back(normed_cot)[0].astype(jnp.bfloat16)
    both = jnp.concatenate([key_cot, value_cot], axis=1)
    kv_term = jnp.dot(normed.T, both, preferred_element_type=jnp.float32)
    return (attended, patch_grad, kv_term)

def reference(patches, latents, gain, w_query, w_key, w_value, w_out, cotangent):

    def step(items):
        return one_video(items[0], items[1], gain, w_query, w_key, w_value, w_out, items[2])
    attended, patch_grad, kv_terms = lax.map(step, (patches, latents, cotangent))
    return (attended, patch_grad, lax.optimization_barrier(jnp.sum(kv_terms, axis=0)))
```

```python
import functools

import jax
import jax.numpy as jnp
from jax import lax
from jax.experimental import pallas as pl
from jax.experimental.pallas import tpu as pltpu
from jax.sharding import Mesh, PartitionSpec as P

HEADS = 16
BLOCK = 9
CHUNK = 40
F32, BF16 = jnp.float32, jnp.bfloat16


def dot(a, b, ca=1, cb=0):
    return lax.dot_general(a, b, (((ca,), (cb,)), ((), ())), preferred_element_type=F32)


def shift(value, axis, step):
    n = lax.axis_size(axis)
    return lax.ppermute(value, axis, [(i, (i + step) % n) for i in range(n)])


def spread(part, width):
    columns = part.shape[1]
    nlat = columns // HEADS
    row = lax.broadcasted_iota(jnp.int32, (HEADS * width, columns), 0) // width
    col = lax.broadcasted_iota(jnp.int32, (HEADS * width, columns), 1) // nlat
    return jnp.where(row == col, jnp.tile(part, (HEADS, 1)), 0.0).astype(BF16)


def by_head(flat, width):
    nlat = flat.shape[1]
    return flat.reshape(HEADS, width, nlat).transpose(1, 0, 2).reshape(width, HEADS * nlat)


def chosen_rows(d):
    v, y, x, c = (lax.axis_index(a) for a in ("v", "y", "x", "c"))
    at = lax.broadcasted_iota(jnp.int32, (32 * CHUNK, 1), 0)
    place, inner = at // CHUNK, at % CHUNK
    dv, i = inner // BLOCK, inner % BLOCK
    dc, dx, dy = place // 16, (place // 4) % 4, place % 4
    owner = ((((v + dv) % 4) * 4 + (y + dy) % 4) * 4 + (x + dx) % 4) * 2 + (c + dc) % 2
    row = jnp.where(inner < 4 * BLOCK, owner * BLOCK + i, -1)
    return (row == lax.broadcasted_iota(jnp.int32, (32 * CHUNK, d), 1)).astype(BF16)


def merge(parts, top_row):
    tops = [p[top_row : top_row + 1] for p in parts]
    top = tops[0]
    for t in tops[1:]:
        top = jnp.maximum(top, t)
    total = sum(p * jnp.exp(t - top) for p, t in zip(parts, tops))
    row = lax.broadcasted_iota(jnp.int32, total.shape, 0)
    return jnp.where(row == top_row, top, total)


def after(value, *others):
    return lax.optimization_barrier((value, *others))[0]


STEP = 256
GROUP = 4
WINDOW = 384


def group(j, width, nlat):
    start = GROUP * width * j // 128 * 128
    return slice(start, start + WINDOW), slice(GROUP * nlat * j, GROUP * nlat * (j + 1))


def call(body, steps, ins, outs, scratch, flops, moved, name):
    specs = [
        pl.BlockSpec(b, m, pipeline_mode=pl.Buffered(1)) if m is whole_block else pl.BlockSpec(b, m)
        for _, b, m in ins
    ]
    return pl.pallas_call(
        body,
        grid=(steps,),
        in_specs=specs,
        out_specs=[pl.BlockSpec(b, m) for _, _, b, m in outs],
        out_shape=[jax.ShapeDtypeStruct(s, t) for s, t, _, _ in outs],
        scratch_shapes=scratch,
        compiler_params=pltpu.CompilerParams(vmem_limit_bytes=56 * 2**20),
        cost_estimate=pl.CostEstimate(flops=flops, bytes_accessed=moved, transcendentals=0),
        name=name,
    )(*[a for a, _, _ in ins])


def whole_block(i):
    return (0, 0)


def row_block(i):
    return (i, 0)


def col_block(i):
    return (0, i)


def softmax_kernel(
    rows,
    width,
    nlat,
    x_ref,
    gain_ref,
    wk_ref,
    wv_ref,
    sq_ref,
    n_ref,
    v_ref,
    e_ref,
    pack_ref,
    s_all,
    v_all,
    acc_ref,
    state_ref,
):
    step, steps = pl.program_id(0), pl.num_programs(0) // 2
    at = pl.multiple_of((step % steps) * STEP, STEP)
    here = pl.ds(at, STEP)

    def valid(columns):
        return lax.broadcasted_iota(jnp.int32, (STEP, columns), 0) + at < rows

    @pl.when(step == 0)
    def _():
        acc_ref[...] = jnp.zeros_like(acc_ref)
        row = lax.broadcasted_iota(jnp.int32, state_ref.shape, 0)
        state_ref[...] = jnp.where(row == 0, -jnp.inf, 0.0)

    @pl.when(step < steps)
    def _():
        x = x_ref[...].astype(F32)
        centred = x - jnp.mean(x, axis=-1, keepdims=True)
        rstd = lax.rsqrt(jnp.mean(centred * centred, axis=-1, keepdims=True) + 1e-06)
        normed = centred * rstd * gain_ref[...].astype(F32)
        normed = jnp.where(valid(x.shape[1]), normed, 0.0).astype(BF16)
        n_ref[...] = normed
        keys = dot(normed, wk_ref[...]).astype(BF16)
        values = dot(normed, wv_ref[...]).astype(BF16)
        v_ref[...] = values
        v_all[here, :] = values
        for j in range(HEADS // GROUP):
            feat, cols = group(j, width, nlat)
            s = dot(keys[:, feat], sq_ref[feat, cols]) * (1.0 / width**0.5)
            s = jnp.where(valid(s.shape[1]), s, -jnp.inf)
            s_all[here, cols] = s
            state_ref[0:1, cols] = jnp.maximum(
                state_ref[0:1, cols], jnp.max(s, axis=0, keepdims=True)
            )

    @pl.when(step >= steps)
    def _():
        for j in range(HEADS // GROUP):
            feat, cols = group(j, width, nlat)
            e = jnp.exp(s_all[here, cols] - state_ref[0:1, cols])
            state_ref[1:2, cols] += jnp.sum(e, axis=0, keepdims=True)
            e = e.astype(BF16)
            e_ref[:, cols] = e
            acc_ref[j] += dot(v_all[here, feat], e, 0, 0)

    @pl.when(step == 2 * steps - 1)
    def _():
        for j in range(HEADS // GROUP):
            feat, cols = group(j, width, nlat)
            lane = lax.broadcasted_iota(jnp.int32, (width, GROUP * nlat), 1) // nlat
            out = jnp.zeros((width, GROUP * nlat), F32)
            for g in range(GROUP):
                start = (GROUP * j + g) * width - feat.start
                out = out + jnp.where(lane == g, acc_ref[j, start : start + width, :], 0.0)
            pack_ref[:width, cols] = out
        pack_ref[width:, :] = state_ref[...]


def grad_kernel(width, nlat, v_ref, sl_ref, e_ref, state_ref, t_ref, d_ref, keep_ref, send_ref):
    @pl.when(pl.program_id(0) == 0)
    def _():
        keep_ref[...] = jnp.zeros_like(keep_ref)
        send_ref[...] = jnp.zeros_like(send_ref)

    for j in range(HEADS // GROUP):
        feat, cols = group(j, width, nlat)
        dprob = dot(v_ref[:, feat], sl_ref[feat, cols])
        grad = e_ref[:, cols].astype(F32) * (dprob - state_ref[0:1, cols]) * state_ref[1:2, cols]
        d_ref[:, cols] = grad.astype(BF16)
    half = keep_ref.shape[0]
    keep_ref[...] += dot(t_ref[:half, :], d_ref[...])
    send_ref[...] += dot(t_ref[half:, :], d_ref[...])


def back_kernel(d_ref, e_ref, qk_ref, qv_ref, state_ref, x_ref, gain_ref, out_ref, scaled_ref):
    @pl.when(pl.program_id(0) == 0)
    def _():
        scaled_ref[...] = (qv_ref[...].astype(F32) * state_ref[2:3, :]).astype(BF16)

    normed_cot = dot(d_ref[...], qk_ref[...], 1, 1) + dot(e_ref[...], scaled_ref[...], 1, 1)
    x = x_ref[...].astype(F32)
    centred = x - jnp.mean(x, axis=-1, keepdims=True)
    rstd = lax.rsqrt(jnp.mean(centred * centred, axis=-1, keepdims=True) + 1e-06)
    xhat = centred * rstd
    dxhat = normed_cot * gain_ref[...].astype(F32)
    mean = jnp.mean(dxhat, axis=-1, keepdims=True)
    slope = jnp.mean(dxhat * xhat, axis=-1, keepdims=True)
    out_ref[...] = ((dxhat - mean - xhat * slope) * rstd).astype(BF16)


def split_kernel(keep_ref, got_ref, *outs):
    for k in range(4):
        for n in range(4):
            place = slice((4 * k + n) * CHUNK, (4 * k + n + 1) * CHUNK)
            outs[n][k * CHUNK : (k + 1) * CHUNK, :] = keep_ref[place, :] + got_ref[place, :]


def per_device(patches, latents, gain, w_query, w_key, w_value, w_out, cotangent):
    core = lax.axis_index("c")
    frames, latent_rows = patches[0], latents[0]
    rows, d = frames.shape
    nlat = latent_rows.shape[0]
    width = d // HEADS
    scale = 1.0 / width**0.5
    cols = HEADS * nlat
    steps = -(-rows // STEP)
    padded = steps * STEP
    half_rows = 16 * CHUNK
    gain_row = gain.reshape(1, d)

    def own_half(value):
        return lax.dynamic_slice_in_dim(value, core * (cols // 2), cols // 2, 1)

    def whole(half, other):
        return jnp.where(
            core == 0, jnp.concatenate([half, other], 1), jnp.concatenate([other, half], 1)
        )

    lc = by_head(dot(w_out, cotangent[0], 1, 1), width)
    lc = own_half(lc + shift(lc, "c", 1))

    query = dot(w_query, latent_rows, 0, 1).astype(BF16)
    spread_q = spread(by_head(query, width).astype(F32), width)
    frames_1, spread_1 = lax.optimization_barrier((frames, spread_q, lc))[:2]
    lc_y = [shift(lc, "y", k) for k in (1, 2, 3)]

    def first(i):
        return (jnp.minimum(i, steps - 1), 0)

    def second(i):
        return (jnp.maximum(i - steps, 0), 0)

    normed, values, expo, pack = call(
        functools.partial(softmax_kernel, rows, width, nlat),
        2 * steps,
        [
            (frames_1, (STEP, d), first),
            (gain_row, (1, d), whole_block),
            (w_key, (d, d), whole_block),
            (w_value, (d, d), whole_block),
            (spread_1, (d, cols), whole_block),
        ],
        [
            ((padded, d), BF16, (STEP, d), first),
            ((padded, d), BF16, (STEP, d), first),
            ((padded, cols), BF16, (STEP, cols), second),
            ((width + 8, cols), F32, (width + 8, cols), whole_block),
        ],
        [
            pltpu.VMEM((padded, cols), F32),
            pltpu.VMEM((padded, d), BF16),
            pltpu.VMEM((HEADS // GROUP, WINDOW, GROUP * nlat), F32),
            pltpu.VMEM((8, cols), F32),
        ],
        4 * padded * (d * d + WINDOW * cols),
        6 * padded * d + 2 * padded * cols + 2 * d * (2 * d + cols),
        "softmax",
    )
    lc = sum(lc_y, after(lc, pack))
    pack = after(pack, lc)
    paired = shift(pack, "c", 1)
    top, top_pair = pack[width : width + 1], paired[width : width + 1]
    top2 = jnp.maximum(top, top_pair)
    half = own_half(merge([pack, paired], width))

    turned = dot(chosen_rows(d), after(normed, half), 1, 1).astype(BF16)
    half = jnp.concatenate([half, jnp.tile(top2.reshape(2, cols // 2), (4, 1)), lc], axis=0)
    halves = [half] + [shift(half, "x", k) for k in (1, 2, 3)]
    tops = [h[width + 8 : width + 10].reshape(1, cols) for h in halves]
    top3 = jnp.maximum(jnp.maximum(tops[0], tops[1]), jnp.maximum(tops[2], tops[3]))
    halves[0] = after(halves[0], turned)
    half = merge([h[: width + 8] for h in halves], width)
    lc = sum(h[width + 16 :] for h in halves)
    lc = whole(lc, shift(lc, "c", 1))
    spread_lc = spread(lc, width)

    half_y = [shift(half, "y", k) for k in (1, 2, 3)]
    u_send = dot(turned[half_rows:], after(expo, half))
    u_got = shift(u_send, "c", 1)
    u = dot(turned[:half_rows], after(expo, u_send))
    half = merge([after(half, u, spread_lc)] + half_y, width)
    pack = whole(half, shift(half, "c", 1))
    gtop, gtotal = pack[width : width + 1], pack[width + 1 : width + 2]
    attn = pack[:width] / gtotal
    factor = jnp.exp(top - gtop) / gtotal
    drift = jnp.sum(lc * attn, axis=0, keepdims=True)
    state = jnp.concatenate([drift, factor * scale, factor, jnp.zeros((5, cols), F32)], axis=0)

    dscore, w, w_send = call(
        functools.partial(grad_kernel, width, nlat),
        steps,
        [
            (values, (STEP, d), row_block),
            (spread_lc, (d, cols), whole_block),
            (expo, (STEP, cols), row_block),
            (state, (8, cols), whole_block),
            (turned, (2 * half_rows, STEP), col_block),
        ],
        [
            ((padded, cols), BF16, (STEP, cols), row_block),
            ((half_rows, cols), F32, (half_rows, cols), whole_block),
            ((half_rows, cols), F32, (half_rows, cols), whole_block),
        ],
        [],
        2 * padded * cols * (WINDOW + 2 * half_rows),
        2 * padded * (2 * d + 2 * cols) + 12 * half_rows * cols,
        "gradient",
    )
    w_got = shift(w_send, "c", 1)
    u = after(u, w_send) * jnp.exp(top - top2) + u_got * jnp.exp(top_pair - top2)
    u = u.reshape(4, 4, CHUNK, cols)
    u_x = [shift(u[k], "x", k) for k in (1, 2, 3)]
    cut = jax.ShapeDtypeStruct((4 * CHUNK, cols), F32)
    parts = pl.pallas_call(
        split_kernel,
        out_shape=[cut] * 4,
        compiler_params=pltpu.CompilerParams(vmem_limit_bytes=56 * 2**20),
        cost_estimate=pl.CostEstimate(
            flops=half_rows * cols, bytes_accessed=12 * half_rows * cols, transcendentals=0
        ),
        name="split",
    )(w, w_got)


    q_key = dot(after(w_key, parts[0]), spread_q).astype(BF16)
    q_value = dot(after(w_value, parts[0]), spread_lc).astype(BF16)
    patch_grad = call(
        back_kernel,
        steps,
        [
            (after(dscore, parts[0]), (STEP, cols), row_block),
            (expo, (STEP, cols), row_block),
            (q_key, (d, cols), whole_block),
            (q_value, (d, cols), whole_block),
            (state, (8, cols), whole_block),
            (frames, (STEP, d), row_block),
            (gain_row, (1, d), whole_block),
        ],
        [((rows, d), BF16, (STEP, d), row_block)],
        [pltpu.VMEM((d, cols), BF16)],
        4 * padded * d * cols,
        4 * padded * (d + cols) + 4 * d * cols,
        "back",
    )[0]
    attn_rows = attn.reshape(width, HEADS, nlat).transpose(1, 0, 2).reshape(d, nlat).astype(BF16)
    attended = dot(attn_rows, w_out, 0, 0).astype(BF16)

    u = after(u[0], patch_grad) * jnp.exp(tops[0] - top3) + sum(
        u_x[k - 1] * jnp.exp(tops[k] - top3) for k in (1, 2, 3)
    )
    u = u * (jnp.exp(top3 - gtop) / gtotal)
    w = after(parts[0], patch_grad)
    w = w + shift(parts[1], "y", 1) + shift(parts[2], "y", 2) + shift(parts[3], "y", 3)
    w = w.reshape(4, CHUNK, cols)
    w = w[0] + shift(w[1], "x", 1) + shift(w[2], "x", 2) + shift(w[3], "x", 3)
    u = u[0] + shift(u[1], "y", 1) + shift(u[2], "y", 2) + shift(u[3], "y", 3)
    kv = jnp.concatenate(
        [dot(w.astype(BF16), spread_q, 1, 1), dot(u.astype(BF16), spread_lc, 1, 1)], axis=1
    )
    kv = [kv[k * BLOCK : (k + 1) * BLOCK] for k in range(4)]
    kv_grad = kv[0] + shift(kv[1], "v", 1) + shift(kv[2], "v", 2) + shift(kv[3], "v", 3)
    return (attended[None], patch_grad[None], kv_grad)


def solution(mesh):
    grid = Mesh(mesh.devices.reshape(4, 4, 4, 2), ("v", "y", "x", "c"))
    frame = ("y", "x", "c")
    return jax.shard_map(
        per_device,
        mesh=grid,
        in_specs=(
            P("v", frame, None),
            P("v", None, None),
            P(),
            P(),
            P(),
            P(),
            P(None, frame),
            P("v", None, frame),
        ),
        out_specs=(
            P("v", None, frame),
            P("v", frame, None),
            P(("v", "y", "x", "c"), None),
        ),
        check_vma=False,
    )
```

```python
import functools

import jax
import jax.numpy as jnp
from jax import lax
from jax.experimental import pallas as pl
from jax.experimental.pallas import tpu as pltpu
from jax.sharding import Mesh, PartitionSpec as P

HEADS = 16
BLOCK = 9
CHUNK = 40
F32, BF16 = jnp.float32, jnp.bfloat16


def dot(a, b, ca=1, cb=0):
    return lax.dot_general(a, b, (((ca,), (cb,)), ((), ())), preferred_element_type=F32)


def shift(value, axis, step):
    n = lax.axis_size(axis)
    return lax.ppermute(value, axis, [(i, (i + step) % n) for i in range(n)])


def spread(part, width):
    columns = part.shape[1]
    nlat = columns // HEADS
    row = lax.broadcasted_iota(jnp.int32, (HEADS * width, columns), 0) // width
    col = lax.broadcasted_iota(jnp.int32, (HEADS * width, columns), 1) // nlat
    return jnp.where(row == col, jnp.tile(part, (HEADS, 1)), 0.0).astype(BF16)


def by_head(flat, width):
    nlat = flat.shape[1]
    return flat.reshape(HEADS, width, nlat).transpose(1, 0, 2).reshape(width, HEADS * nlat)


def chosen_rows(d):
    v, y, x, c = (lax.axis_index(a) for a in ("v", "y", "x", "c"))
    at = lax.broadcasted_iota(jnp.int32, (32 * CHUNK, 1), 0)
    place, inner = at // CHUNK, at % CHUNK
    dv, i = inner // BLOCK, inner % BLOCK
    dc, dx, dy = place // 16, (place // 4) % 4, place % 4
    owner = ((((v + dv) % 4) * 4 + (y + dy) % 4) * 4 + (x + dx) % 4) * 2 + (c + dc) % 2
    row = jnp.where(inner < 4 * BLOCK, owner * BLOCK + i, -1)
    return (row == lax.broadcasted_iota(jnp.int32, (32 * CHUNK, d), 1)).astype(BF16)


def merge(parts, top_row):
    tops = [p[top_row : top_row + 1] for p in parts]
    top = tops[0]
    for t in tops[1:]:
        top = jnp.maximum(top, t)
    total = sum(p * jnp.exp(t - top) for p, t in zip(parts, tops))
    row = lax.broadcasted_iota(jnp.int32, total.shape, 0)
    return jnp.where(row == top_row, top, total)


def after(value, *others):
    return lax.optimization_barrier((value, *others))[0]


STEP = 256
LONG = 512
GROUP = 4
WINDOW = 384


def group(j, width, nlat):
    start = GROUP * width * j // 128 * 128
    return slice(start, start + WINDOW), slice(GROUP * nlat * j, GROUP * nlat * (j + 1))


def call(body, steps, ins, outs, scratch, flops, moved, name):
    specs = [
        pl.BlockSpec(b, m, pipeline_mode=pl.Buffered(1)) if m is whole_block else pl.BlockSpec(b, m)
        for _, b, m in ins
    ]
    return pl.pallas_call(
        body,
        grid=(steps,),
        in_specs=specs,
        out_specs=[pl.BlockSpec(b, m) for _, _, b, m in outs],
        out_shape=[jax.ShapeDtypeStruct(s, t) for s, t, _, _ in outs],
        scratch_shapes=scratch,
        compiler_params=pltpu.CompilerParams(vmem_limit_bytes=56 * 2**20),
        cost_estimate=pl.CostEstimate(flops=flops, bytes_accessed=moved, transcendentals=0),
        name=name,
    )(*[a for a, _, _ in ins])


def whole_block(i):
    return (0, 0)


def row_block(i):
    return (i, 0)


def col_block(i):
    return (0, i)


def softmax_kernel(
    rows,
    width,
    nlat,
    x_ref,
    gain_ref,
    wk_ref,
    wv_ref,
    wq_ref,
    lat_ref,
    n_ref,
    v_ref,
    e_ref,
    pack_ref,
    sq_ref,
    s_all,
    n_all,
    acc_ref,
    state_ref,
):
    step, steps = pl.program_id(0), pl.num_programs(0) // 2
    at = pl.multiple_of((step % steps) * STEP, STEP)
    here = pl.ds(at, STEP)

    def valid(columns):
        return lax.broadcasted_iota(jnp.int32, (STEP, columns), 0) + at < rows

    @pl.when(step == 0)
    def _():
        acc_ref[...] = jnp.zeros_like(acc_ref)
        row = lax.broadcasted_iota(jnp.int32, state_ref.shape, 0)
        state_ref[...] = jnp.where(row == 0, -jnp.inf, 0.0)
        twice = jnp.concatenate([lat_ref[...], lat_ref[...]], axis=0)
        query = dot(twice, wq_ref[...]).astype(BF16).astype(F32).T
        sq_ref[...] = jnp.zeros_like(sq_ref)
        head_row = lax.broadcasted_iota(jnp.int32, (2 * width, 2 * nlat), 0) // width
        head_col = lax.broadcasted_iota(jnp.int32, (2 * width, 2 * nlat), 1) // nlat
        for t in range(HEADS // 2):
            feat, cols = slice(2 * width * t, 2 * width * (t + 1)), slice(2 * nlat * t, 2 * nlat * (t + 1))
            sq_ref[feat, cols] = jnp.where(head_row == head_col, query[feat, :], 0.0).astype(BF16)

    @pl.when(step < steps)
    def _():
        x = x_ref[...].astype(F32)
        centred = x - jnp.mean(x, axis=-1, keepdims=True)
        rstd = lax.rsqrt(jnp.mean(centred * centred, axis=-1, keepdims=True) + 1e-06)
        normed = centred * rstd * gain_ref[...].astype(F32)[None, :]
        normed = jnp.where(valid(x.shape[1]), normed, 0.0).astype(BF16)
        n_ref[...] = normed
        keys = dot(normed, wk_ref[...]).astype(BF16)
        n_all[here, :] = normed
        for j in range(HEADS // GROUP):
            feat, cols = group(j, width, nlat)
            s = dot(keys[:, feat], sq_ref[feat, cols]) * (1.0 / width**0.5)
            s = jnp.where(valid(s.shape[1]), s, -jnp.inf)
            s_all[here, cols] = s
            state_ref[0:1, cols] = jnp.maximum(
                state_ref[0:1, cols], jnp.max(s, axis=0, keepdims=True)
            )

    @pl.when(step >= steps)
    def _():
        values = dot(n_all[here, :], wv_ref[...]).astype(BF16)
        v_ref[...] = values
        for j in range(HEADS // GROUP):
            feat, cols = group(j, width, nlat)
            e = jnp.exp(s_all[here, cols] - state_ref[0:1, cols])
            state_ref[1:2, cols] += jnp.sum(e, axis=0, keepdims=True)
            e = e.astype(BF16)
            e_ref[:, cols] = e
            acc_ref[j] += dot(values[:, feat], e, 0, 0)

    @pl.when(step == 2 * steps - 1)
    def _():
        for j in range(HEADS // GROUP):
            feat, cols = group(j, width, nlat)
            lane = lax.broadcasted_iota(jnp.int32, (width, GROUP * nlat), 1) // nlat
            out = jnp.zeros((width, GROUP * nlat), F32)
            for g in range(GROUP):
                start = (GROUP * j + g) * width - feat.start
                out = out + jnp.where(lane == g, acc_ref[j, start : start + width, :], 0.0)
            pack_ref[:width, cols] = out
        pack_ref[width:, :] = state_ref[...]


def grad_kernel(width, nlat, v_ref, sl_ref, e_ref, state_ref, t_ref, d_ref, keep_ref, send_ref):
    @pl.when(pl.program_id(0) == 0)
    def _():
        keep_ref[...] = jnp.zeros_like(keep_ref)
        send_ref[...] = jnp.zeros_like(send_ref)

    for j in range(HEADS // GROUP):
        feat, cols = group(j, width, nlat)
        dprob = dot(v_ref[:, feat], sl_ref[feat, cols])
        grad = e_ref[:, cols].astype(F32) * (dprob - state_ref[0:1, cols]) * state_ref[1:2, cols]
        d_ref[:, cols] = grad.astype(BF16)
    half = keep_ref.shape[0]
    keep_ref[...] += dot(t_ref[:half, :], d_ref[...])
    send_ref[...] += dot(t_ref[half:, :], d_ref[...])


def back_kernel(d_ref, e_ref, qk_ref, qv_ref, state_ref, x_ref, gain_ref, out_ref, scaled_ref):
    @pl.when(pl.program_id(0) == 0)
    def _():
        scaled_ref[...] = (qv_ref[...].astype(F32) * state_ref[2:3, :]).astype(BF16)

    normed_cot = dot(d_ref[...], qk_ref[...], 1, 1) + dot(e_ref[...], scaled_ref[...], 1, 1)
    x = x_ref[...].astype(F32)
    centred = x - jnp.mean(x, axis=-1, keepdims=True)
    rstd = lax.rsqrt(jnp.mean(centred * centred, axis=-1, keepdims=True) + 1e-06)
    xhat = centred * rstd
    dxhat = normed_cot * gain_ref[...].astype(F32)[None, :]
    mean = jnp.mean(dxhat, axis=-1, keepdims=True)
    slope = jnp.mean(dxhat * xhat, axis=-1, keepdims=True)
    out_ref[...] = ((dxhat - mean - xhat * slope) * rstd).astype(BF16)


def split_kernel(keep_ref, got_ref, *outs):
    for k in range(4):
        for n in range(4):
            place = slice((4 * k + n) * CHUNK, (4 * k + n + 1) * CHUNK)
            outs[n][k * CHUNK : (k + 1) * CHUNK, :] = keep_ref[place, :] + got_ref[place, :]


def per_device(patches, latents, gain, w_query, w_key, w_value, w_out, cotangent):
    core = lax.axis_index("c")
    frames, latent_rows = patches[0], latents[0]
    rows, d = frames.shape
    nlat = latent_rows.shape[0]
    width = d // HEADS
    scale = 1.0 / width**0.5
    cols = HEADS * nlat
    steps = -(-rows // STEP)
    padded = steps * STEP
    half_rows = 16 * CHUNK

    def own_half(value):
        return lax.dynamic_slice_in_dim(value, core * (cols // 2), cols // 2, 1)

    def whole(half, other):
        return jnp.where(
            core == 0, jnp.concatenate([half, other], 1), jnp.concatenate([other, half], 1)
        )

    lc = by_head(dot(w_out, cotangent[0], 1, 1), width)
    lc = own_half(lc + shift(lc, "c", 1))

    frames_1 = after(frames, lc)
    lc_y = [shift(lc, "y", k) for k in (1, 2, 3)]

    def first(i):
        return (jnp.minimum(i, steps - 1), 0)

    def second(i):
        return (jnp.maximum(i - steps, 0), 0)

    normed, values, expo, pack, spread_q = call(
        functools.partial(softmax_kernel, rows, width, nlat),
        2 * steps,
        [
            (frames_1, (STEP, d), first),
            (gain, (d,), lambda i: (0,)),
            (w_key, (d, d), whole_block),
            (w_value, (d, d), whole_block),
            (w_query, (d, d), whole_block),
            (latent_rows, (nlat, d), whole_block),
        ],
        [
            ((padded, d), BF16, (STEP, d), first),
            ((padded, d), BF16, (STEP, d), second),
            ((padded, cols), BF16, (STEP, cols), second),
            ((width + 8, cols), F32, (width + 8, cols), whole_block),
            ((d, cols), BF16, (d, cols), whole_block),
        ],
        [
            pltpu.VMEM((padded, cols), F32),
            pltpu.VMEM((padded, d), BF16),
            pltpu.VMEM((HEADS // GROUP, WINDOW, GROUP * nlat), F32),
            pltpu.VMEM((8, cols), F32),
        ],
        4 * padded * (d * d + WINDOW * cols),
        6 * padded * d + 2 * padded * cols + 2 * d * (2 * d + cols),
        "softmax",
    )
    lc = sum(lc_y, after(lc, pack))
    pack = after(pack, lc)
    paired = shift(pack, "c", 1)
    top, top_pair = pack[width : width + 1], paired[width : width + 1]
    top2 = jnp.maximum(top, top_pair)
    half = own_half(merge([pack, paired], width))

    turned = dot(chosen_rows(d), after(normed, half), 1, 1).astype(BF16)
    half = jnp.concatenate([half, jnp.tile(top2.reshape(2, cols // 2), (4, 1)), lc], axis=0)
    halves = [half] + [shift(half, "x", k) for k in (1, 2, 3)]
    tops = [h[width + 8 : width + 10].reshape(1, cols) for h in halves]
    top3 = jnp.maximum(jnp.maximum(tops[0], tops[1]), jnp.maximum(tops[2], tops[3]))
    q_key = dot(after(w_key, turned), spread_q).astype(BF16)
    halves[0] = after(halves[0], q_key)
    half = merge([h[: width + 8] for h in halves], width)
    lc = sum(h[width + 16 :] for h in halves)
    lc = whole(lc, shift(lc, "c", 1))
    spread_lc = spread(lc, width)

    half_y = [shift(half, "y", k) for k in (1, 2, 3)]
    u_send = dot(turned[half_rows:], after(expo, half))
    u_got = shift(u_send, "c", 1)
    u = dot(turned[:half_rows], after(expo, u_send))
    half = merge([after(half, u, spread_lc)] + half_y, width)
    pack = whole(half, shift(half, "c", 1))
    gtop, gtotal = pack[width : width + 1], pack[width + 1 : width + 2]
    attn = pack[:width] / gtotal
    factor = jnp.exp(top - gtop) / gtotal
    drift = jnp.sum(lc * attn, axis=0, keepdims=True)
    state = jnp.concatenate([drift, factor * scale, factor, jnp.zeros((5, cols), F32)], axis=0)

    dscore, w, w_send = call(
        functools.partial(grad_kernel, width, nlat),
        padded // LONG,
        [
            (values, (LONG, d), row_block),
            (spread_lc, (d, cols), whole_block),
            (expo, (LONG, cols), row_block),
            (state, (8, cols), whole_block),
            (turned, (2 * half_rows, LONG), col_block),
        ],
        [
            ((padded, cols), BF16, (LONG, cols), row_block),
            ((half_rows, cols), F32, (half_rows, cols), whole_block),
            ((half_rows, cols), F32, (half_rows, cols), whole_block),
        ],
        [],
        2 * padded * cols * (WINDOW + 2 * half_rows),
        2 * padded * (2 * d + 2 * cols) + 12 * half_rows * cols,
        "gradient",
    )
    w_got = shift(w_send, "c", 1)
    u = after(u, w_send) * jnp.exp(top - top2) + u_got * jnp.exp(top_pair - top2)
    u = u.reshape(4, 4, CHUNK, cols)
    u_x = [shift(u[k], "x", k) for k in (1, 2, 3)]
    cut = jax.ShapeDtypeStruct((4 * CHUNK, cols), F32)
    parts = pl.pallas_call(
        split_kernel,
        out_shape=[cut] * 4,
        compiler_params=pltpu.CompilerParams(vmem_limit_bytes=56 * 2**20),
        cost_estimate=pl.CostEstimate(
            flops=half_rows * cols, bytes_accessed=12 * half_rows * cols, transcendentals=0
        ),
        name="split",
    )(w, w_got)


    q_value = dot(after(w_value, parts[0]), spread_lc).astype(BF16)
    patch_grad = call(
        back_kernel,
        steps,
        [
            (after(dscore, parts[0]), (STEP, cols), row_block),
            (expo, (STEP, cols), row_block),
            (q_key, (d, cols), whole_block),
            (q_value, (d, cols), whole_block),
            (state, (8, cols), whole_block),
            (frames, (STEP, d), row_block),
            (gain, (d,), lambda i: (0,)),
        ],
        [((rows, d), BF16, (STEP, d), row_block)],
        [pltpu.VMEM((d, cols), BF16)],
        4 * padded * d * cols,
        4 * padded * (d + cols) + 4 * d * cols,
        "back",
    )[0]
    attn_rows = attn.reshape(width, HEADS, nlat).transpose(1, 0, 2).reshape(d, nlat).astype(BF16)
    attended = dot(attn_rows, w_out, 0, 0).astype(BF16)

    u = after(u[0], patch_grad) * jnp.exp(tops[0] - top3) + sum(
        u_x[k - 1] * jnp.exp(tops[k] - top3) for k in (1, 2, 3)
    )
    u = u * (jnp.exp(top3 - gtop) / gtotal)
    w = after(parts[0], patch_grad)
    w = w + shift(parts[1], "y", 1) + shift(parts[2], "y", 2) + shift(parts[3], "y", 3)
    w = w.reshape(4, CHUNK, cols)
    w = w[0] + shift(w[1], "x", 1) + shift(w[2], "x", 2) + shift(w[3], "x", 3)
    u = u[0] + shift(u[1], "y", 1) + shift(u[2], "y", 2) + shift(u[3], "y", 3)
    kv = jnp.concatenate(
        [dot(w.astype(BF16), spread_q, 1, 1), dot(u.astype(BF16), spread_lc, 1, 1)], axis=1
    )
    kv = [kv[k * BLOCK : (k + 1) * BLOCK] for k in range(4)]
    kv_grad = kv[0] + shift(kv[1], "v", 1) + shift(kv[2], "v", 2) + shift(kv[3], "v", 3)
    return (attended[None], patch_grad[None], kv_grad)


def solution(mesh):
    grid = Mesh(mesh.devices.reshape(4, 4, 4, 2), ("v", "y", "x", "c"))
    frame = ("y", "x", "c")
    return jax.shard_map(
        per_device,
        mesh=grid,
        in_specs=(
            P("v", frame, None),
            P("v", None, None),
            P(),
            P(),
            P(),
            P(),
            P(None, frame),
            P("v", None, frame),
        ),
        out_specs=(
            P("v", None, frame),
            P("v", frame, None),
            P(("v", "y", "x", "c"), None),
        ),
        check_vma=False,
    )
```

```python
import functools

import jax
import jax.numpy as jnp
from jax import lax
from jax.experimental import pallas as pl
from jax.experimental.pallas import tpu as pltpu
from jax.sharding import Mesh, PartitionSpec as P

HEADS = 16
BLOCK = 9
CHUNK = 40
F32, BF16 = jnp.float32, jnp.bfloat16


def dot(a, b, ca=1, cb=0):
    return lax.dot_general(a, b, (((ca,), (cb,)), ((), ())), preferred_element_type=F32)


def shift(value, axis, step):
    n = lax.axis_size(axis)
    return lax.ppermute(value, axis, [(i, (i + step) % n) for i in range(n)])


def spread(part, width):
    columns = part.shape[1]
    nlat = columns // HEADS
    row = lax.broadcasted_iota(jnp.int32, (HEADS * width, columns), 0) // width
    col = lax.broadcasted_iota(jnp.int32, (HEADS * width, columns), 1) // nlat
    return jnp.where(row == col, jnp.tile(part, (HEADS, 1)), 0.0).astype(BF16)


def by_head(flat, width):
    nlat = flat.shape[1]
    return flat.reshape(HEADS, width, nlat).transpose(1, 0, 2).reshape(width, HEADS * nlat)


def chosen_rows(d):
    v, y, x, c = (lax.axis_index(a) for a in ("v", "y", "x", "c"))
    at = lax.broadcasted_iota(jnp.int32, (32 * CHUNK, 1), 0)
    place, inner = at // CHUNK, at % CHUNK
    dv, i = inner // BLOCK, inner % BLOCK
    dc, dx, dy = place // 16, (place // 4) % 4, place % 4
    owner = ((((v + dv) % 4) * 4 + (y + dy) % 4) * 4 + (x + dx) % 4) * 2 + (c + dc) % 2
    row = jnp.where(inner < 4 * BLOCK, owner * BLOCK + i, -1)
    return (row == lax.broadcasted_iota(jnp.int32, (32 * CHUNK, d), 1)).astype(BF16)


def merge(parts, top_row):
    tops = [p[top_row : top_row + 1] for p in parts]
    top = tops[0]
    for t in tops[1:]:
        top = jnp.maximum(top, t)
    total = sum(p * jnp.exp(t - top) for p, t in zip(parts, tops))
    row = lax.broadcasted_iota(jnp.int32, total.shape, 0)
    return jnp.where(row == top_row, top, total)


def after(value, *others):
    return lax.optimization_barrier((value, *others))[0]


STEP = 256
LONG = 512
GROUP = 4
WINDOW = 384


def group(j, width, nlat):
    start = GROUP * width * j // 128 * 128
    return slice(start, start + WINDOW), slice(GROUP * nlat * j, GROUP * nlat * (j + 1))


def call(body, steps, ins, outs, scratch, flops, moved, name, room):
    specs = [
        pl.BlockSpec(b, m, pipeline_mode=pl.Buffered(1)) if m is whole_block else pl.BlockSpec(b, m)
        for _, b, m in ins
    ]
    return pl.pallas_call(
        body,
        grid=(steps,),
        in_specs=specs,
        out_specs=[pl.BlockSpec(b, m) for _, _, b, m in outs],
        out_shape=[jax.ShapeDtypeStruct(s, t) for s, t, _, _ in outs],
        scratch_shapes=scratch,
        compiler_params=pltpu.CompilerParams(vmem_limit_bytes=room * 2**20),
        cost_estimate=pl.CostEstimate(flops=flops, bytes_accessed=moved, transcendentals=0),
        name=name,
    )(*[a for a, _, _ in ins])


def whole_block(i):
    return (0, 0)


def row_block(i):
    return (i, 0)


def col_block(i):
    return (0, i)


def softmax_kernel(
    rows,
    width,
    nlat,
    x_ref,
    gain_ref,
    wk_ref,
    wv_ref,
    wq_ref,
    lat_ref,
    n_ref,
    v_ref,
    e_ref,
    pack_ref,
    sq_ref,
    s_all,
    n_all,
    acc_ref,
    state_ref,
):
    step, steps = pl.program_id(0), pl.num_programs(0) // 2
    at = pl.multiple_of((step % steps) * STEP, STEP)
    here = pl.ds(at, STEP)

    def valid(columns):
        return lax.broadcasted_iota(jnp.int32, (STEP, columns), 0) + at < rows

    @pl.when(step == 0)
    def _():
        acc_ref[...] = jnp.zeros_like(acc_ref)
        row = lax.broadcasted_iota(jnp.int32, state_ref.shape, 0)
        state_ref[...] = jnp.where(row == 0, -jnp.inf, 0.0)
        twice = jnp.concatenate([lat_ref[...], lat_ref[...]], axis=0)
        query = dot(twice, wq_ref[...]).astype(BF16).astype(F32).T
        sq_ref[...] = jnp.zeros_like(sq_ref)
        head_row = lax.broadcasted_iota(jnp.int32, (2 * width, 2 * nlat), 0) // width
        head_col = lax.broadcasted_iota(jnp.int32, (2 * width, 2 * nlat), 1) // nlat
        for t in range(HEADS // 2):
            feat, cols = slice(2 * width * t, 2 * width * (t + 1)), slice(2 * nlat * t, 2 * nlat * (t + 1))
            sq_ref[feat, cols] = jnp.where(head_row == head_col, query[feat, :], 0.0).astype(BF16)

    @pl.when(step < steps)
    def _():
        x = x_ref[...].astype(F32)
        centred = x - jnp.mean(x, axis=-1, keepdims=True)
        rstd = lax.rsqrt(jnp.mean(centred * centred, axis=-1, keepdims=True) + 1e-06)
        normed = centred * rstd * gain_ref[...].astype(F32)[None, :]
        normed = jnp.where(valid(x.shape[1]), normed, 0.0).astype(BF16)
        n_ref[...] = normed
        keys = dot(normed, wk_ref[...]).astype(BF16)
        n_all[here, :] = normed
        for j in range(HEADS // GROUP):
            feat, cols = group(j, width, nlat)
            s = dot(keys[:, feat], sq_ref[feat, cols]) * (1.0 / width**0.5)
            s = jnp.where(valid(s.shape[1]), s, -jnp.inf)
            s_all[here, cols] = s
            state_ref[0:1, cols] = jnp.maximum(
                state_ref[0:1, cols], jnp.max(s, axis=0, keepdims=True)
            )

    @pl.when(step >= steps)
    def _():
        values = dot(n_all[here, :], wv_ref[...]).astype(BF16)
        v_ref[...] = values
        for j in range(HEADS // GROUP):
            feat, cols = group(j, width, nlat)
            e = jnp.exp(s_all[here, cols] - state_ref[0:1, cols])
            state_ref[1:2, cols] += jnp.sum(e, axis=0, keepdims=True)
            e = e.astype(BF16)
            e_ref[:, cols] = e
            acc_ref[j] += dot(values[:, feat], e, 0, 0)

    @pl.when(step == 2 * steps - 1)
    def _():
        for j in range(HEADS // GROUP):
            feat, cols = group(j, width, nlat)
            lane = lax.broadcasted_iota(jnp.int32, (width, GROUP * nlat), 1) // nlat
            out = jnp.zeros((width, GROUP * nlat), F32)
            for g in range(GROUP):
                start = (GROUP * j + g) * width - feat.start
                out = out + jnp.where(lane == g, acc_ref[j, start : start + width, :], 0.0)
            pack_ref[:width, cols] = out
        pack_ref[width:, :] = state_ref[...]


def grad_kernel(width, nlat, v_ref, sl_ref, e_ref, state_ref, t_ref, d_ref, keep_ref, send_ref):
    @pl.when(pl.program_id(0) == 0)
    def _():
        keep_ref[...] = jnp.zeros_like(keep_ref)
        send_ref[...] = jnp.zeros_like(send_ref)

    for j in range(HEADS // GROUP):
        feat, cols = group(j, width, nlat)
        dprob = dot(v_ref[:, feat], sl_ref[feat, cols])
        grad = e_ref[:, cols].astype(F32) * (dprob - state_ref[0:1, cols]) * state_ref[1:2, cols]
        d_ref[:, cols] = grad.astype(BF16)
    half = keep_ref.shape[0]
    keep_ref[...] += dot(t_ref[:half, :], d_ref[...])
    send_ref[...] += dot(t_ref[half:, :], d_ref[...])


def back_kernel(d_ref, e_ref, qk_ref, qv_ref, state_ref, x_ref, gain_ref, out_ref, scaled_ref):
    @pl.when(pl.program_id(0) == 0)
    def _():
        scaled_ref[...] = (qv_ref[...].astype(F32) * state_ref[2:3, :]).astype(BF16)

    normed_cot = dot(d_ref[...], qk_ref[...], 1, 1) + dot(e_ref[...], scaled_ref[...], 1, 1)
    x = x_ref[...].astype(F32)
    centred = x - jnp.mean(x, axis=-1, keepdims=True)
    rstd = lax.rsqrt(jnp.mean(centred * centred, axis=-1, keepdims=True) + 1e-06)
    xhat = centred * rstd
    dxhat = normed_cot * gain_ref[...].astype(F32)[None, :]
    mean = jnp.mean(dxhat, axis=-1, keepdims=True)
    slope = jnp.mean(dxhat * xhat, axis=-1, keepdims=True)
    out_ref[...] = ((dxhat - mean - xhat * slope) * rstd).astype(BF16)


def split_kernel(keep_ref, got_ref, *outs):
    for k in range(4):
        for n in range(4):
            place = slice((4 * k + n) * CHUNK, (4 * k + n + 1) * CHUNK)
            outs[n][k * CHUNK : (k + 1) * CHUNK, :] = keep_ref[place, :] + got_ref[place, :]


def per_device(patches, latents, gain, w_query, w_key, w_value, w_out, cotangent):
    core = lax.axis_index("c")
    frames, latent_rows = patches[0], latents[0]
    rows, d = frames.shape
    nlat = latent_rows.shape[0]
    width = d // HEADS
    scale = 1.0 / width**0.5
    cols = HEADS * nlat
    steps = -(-rows // STEP)
    padded = steps * STEP
    half_rows = 16 * CHUNK

    def own_half(value):
        return lax.dynamic_slice_in_dim(value, core * (cols // 2), cols // 2, 1)

    def whole(half, other):
        return jnp.where(
            core == 0, jnp.concatenate([half, other], 1), jnp.concatenate([other, half], 1)
        )

    lc = by_head(dot(w_out, cotangent[0], 1, 1), width)
    lc = own_half(lc + shift(lc, "c", 1))

    frames_1 = after(frames, lc)
    lc_y = [shift(lc, "y", k) for k in (1, 2, 3)]

    def first(i):
        return (jnp.minimum(i, steps - 1), 0)

    def second(i):
        return (jnp.maximum(i - steps, 0), 0)

    normed, values, expo, pack, spread_q = call(
        functools.partial(softmax_kernel, rows, width, nlat),
        2 * steps,
        [
            (frames_1, (STEP, d), first),
            (gain, (d,), lambda i: (0,)),
            (w_key, (d, d), whole_block),
            (w_value, (d, d), whole_block),
            (w_query, (d, d), whole_block),
            (latent_rows, (nlat, d), whole_block),
        ],
        [
            ((padded, d), BF16, (STEP, d), first),
            ((padded, d), BF16, (STEP, d), second),
            ((padded, cols), BF16, (STEP, cols), second),
            ((width + 8, cols), F32, (width + 8, cols), whole_block),
            ((d, cols), BF16, (d, cols), whole_block),
        ],
        [
            pltpu.VMEM((padded, cols), F32),
            pltpu.VMEM((padded, d), BF16),
            pltpu.VMEM((HEADS // GROUP, WINDOW, GROUP * nlat), F32),
            pltpu.VMEM((8, cols), F32),
        ],
        4 * padded * (d * d + WINDOW * cols),
        6 * padded * d + 2 * padded * cols + 2 * d * (2 * d + cols),
        "softmax",
        56,
    )
    lc = sum(lc_y, after(lc, pack))
    pack = after(pack, lc)
    paired = shift(pack, "c", 1)
    top, top_pair = pack[width : width + 1], paired[width : width + 1]
    top2 = jnp.maximum(top, top_pair)
    half = own_half(merge([pack, paired], width))

    turned = dot(chosen_rows(d), after(normed, half), 1, 1).astype(BF16)
    half = jnp.concatenate([half, jnp.tile(top2.reshape(2, cols // 2), (4, 1)), lc], axis=0)
    halves = [half] + [shift(half, "x", k) for k in (1, 2, 3)]
    tops = [h[width + 8 : width + 10].reshape(1, cols) for h in halves]
    top3 = jnp.maximum(jnp.maximum(tops[0], tops[1]), jnp.maximum(tops[2], tops[3]))
    q_key = dot(after(w_key, turned), spread_q).astype(BF16)
    halves[0] = after(halves[0], q_key)
    half = merge([h[: width + 8] for h in halves], width)
    lc = sum(h[width + 16 :] for h in halves)
    lc = whole(lc, shift(lc, "c", 1))
    spread_lc = spread(lc, width)

    half_y = [shift(half, "y", k) for k in (1, 2, 3)]
    u_send = dot(turned[half_rows:], after(expo, half))
    u_got = shift(u_send, "c", 1)
    u = dot(turned[:half_rows], after(expo, u_send))
    half = merge([after(half, u, spread_lc)] + half_y, width)
    pack = whole(half, shift(half, "c", 1))
    gtop, gtotal = pack[width : width + 1], pack[width + 1 : width + 2]
    attn = pack[:width] / gtotal
    factor = jnp.exp(top - gtop) / gtotal
    drift = jnp.sum(lc * attn, axis=0, keepdims=True)
    state = jnp.concatenate([drift, factor * scale, factor, jnp.zeros((5, cols), F32)], axis=0)

    dscore, w, w_send = call(
        functools.partial(grad_kernel, width, nlat),
        padded // LONG,
        [
            (values, (LONG, d), row_block),
            (spread_lc, (d, cols), whole_block),
            (expo, (LONG, cols), row_block),
            (state, (8, cols), whole_block),
            (turned, (2 * half_rows, LONG), col_block),
        ],
        [
            ((padded, cols), BF16, (LONG, cols), row_block),
            ((half_rows, cols), F32, (half_rows, cols), whole_block),
            ((half_rows, cols), F32, (half_rows, cols), whole_block),
        ],
        [],
        2 * padded * cols * (WINDOW + 2 * half_rows),
        2 * padded * (2 * d + 2 * cols) + 12 * half_rows * cols,
        "gradient",
        32,
    )
    w_got = shift(w_send, "c", 1)
    u = after(u, w_send) * jnp.exp(top - top2) + u_got * jnp.exp(top_pair - top2)
    u = u.reshape(4, 4, CHUNK, cols)
    u_x = [shift(u[k], "x", k) for k in (1, 2, 3)]
    cut = jax.ShapeDtypeStruct((4 * CHUNK, cols), F32)
    parts = pl.pallas_call(
        split_kernel,
        out_shape=[cut] * 4,
        compiler_params=pltpu.CompilerParams(vmem_limit_bytes=16 * 2**20),
        cost_estimate=pl.CostEstimate(
            flops=half_rows * cols, bytes_accessed=12 * half_rows * cols, transcendentals=0
        ),
        name="split",
    )(w, w_got)


    q_value = dot(after(w_value, parts[0]), spread_lc).astype(BF16)
    patch_grad = call(
        back_kernel,
        steps,
        [
            (after(dscore, parts[0]), (STEP, cols), row_block),
            (expo, (STEP, cols), row_block),
            (q_key, (d, cols), whole_block),
            (q_value, (d, cols), whole_block),
            (state, (8, cols), whole_block),
            (frames, (STEP, d), row_block),
            (gain, (d,), lambda i: (0,)),
        ],
        [((rows, d), BF16, (STEP, d), row_block)],
        [pltpu.VMEM((d, cols), BF16)],
        4 * padded * d * cols,
        4 * padded * (d + cols) + 4 * d * cols,
        "back",
        28,
    )[0]
    attn_rows = attn.reshape(width, HEADS, nlat).transpose(1, 0, 2).reshape(d, nlat).astype(BF16)
    attended = dot(attn_rows, w_out, 0, 0).astype(BF16)

    u = after(u[0], patch_grad) * jnp.exp(tops[0] - top3) + sum(
        u_x[k - 1] * jnp.exp(tops[k] - top3) for k in (1, 2, 3)
    )
    u = u * (jnp.exp(top3 - gtop) / gtotal)
    w = after(parts[0], patch_grad)
    w = w + shift(parts[1], "y", 1) + shift(parts[2], "y", 2) + shift(parts[3], "y", 3)
    w = w.reshape(4, CHUNK, cols)
    w = w[0] + shift(w[1], "x", 1) + shift(w[2], "x", 2) + shift(w[3], "x", 3)
    u = u[0] + shift(u[1], "y", 1) + shift(u[2], "y", 2) + shift(u[3], "y", 3)
    kv = jnp.concatenate(
        [dot(w.astype(BF16), spread_q, 1, 1), dot(u.astype(BF16), spread_lc, 1, 1)], axis=1
    )
    kv = [kv[k * BLOCK : (k + 1) * BLOCK] for k in range(4)]
    kv_grad = kv[0] + shift(kv[1], "v", 1) + shift(kv[2], "v", 2) + shift(kv[3], "v", 3)
    return (attended[None], patch_grad[None], kv_grad)


def solution(mesh):
    grid = Mesh(mesh.devices.reshape(4, 4, 4, 2), ("v", "y", "x", "c"))
    frame = ("y", "x", "c")
    return jax.shard_map(
        per_device,
        mesh=grid,
        in_specs=(
            P("v", frame, None),
            P("v", None, None),
            P(),
            P(),
            P(),
            P(),
            P(None, frame),
            P("v", None, frame),
        ),
        out_specs=(
            P("v", None, frame),
            P("v", frame, None),
            P(("v", "y", "x", "c"), None),
        ),
        check_vma=False,
    )
```

```python
import functools

import jax
import jax.numpy as jnp
from jax import lax
from jax.experimental import pallas as pl
from jax.experimental.pallas import tpu as pltpu
from jax.sharding import Mesh, PartitionSpec as P

HEADS = 16
BLOCK = 9
CHUNK = 40
F32, BF16 = jnp.float32, jnp.bfloat16


def dot(a, b, ca=1, cb=0):
    return lax.dot_general(a, b, (((ca,), (cb,)), ((), ())), preferred_element_type=F32)


def shift(value, axis, step):
    n = lax.axis_size(axis)
    return lax.ppermute(value, axis, [(i, (i + step) % n) for i in range(n)])


def spread(part, width):
    columns = part.shape[1]
    nlat = columns // HEADS
    row = lax.broadcasted_iota(jnp.int32, (HEADS * width, columns), 0) // width
    col = lax.broadcasted_iota(jnp.int32, (HEADS * width, columns), 1) // nlat
    return jnp.where(row == col, jnp.tile(part, (HEADS, 1)), 0.0).astype(BF16)


def by_head(flat, width):
    nlat = flat.shape[1]
    return flat.reshape(HEADS, width, nlat).transpose(1, 0, 2).reshape(width, HEADS * nlat)


def chosen_rows(d):
    v, y, x, c = (lax.axis_index(a) for a in ("v", "y", "x", "c"))
    at = lax.broadcasted_iota(jnp.int32, (32 * CHUNK, 1), 0)
    place, inner = at // CHUNK, at % CHUNK
    dv, i = inner // BLOCK, inner % BLOCK
    dc, dx, dy = place // 16, (place // 4) % 4, place % 4
    owner = ((((v + dv) % 4) * 4 + (y + dy) % 4) * 4 + (x + dx) % 4) * 2 + (c + dc) % 2
    row = jnp.where(inner < 4 * BLOCK, owner * BLOCK + i, -1)
    return (row == lax.broadcasted_iota(jnp.int32, (32 * CHUNK, d), 1)).astype(BF16)


def merge(parts, top_row):
    tops = [p[top_row : top_row + 1] for p in parts]
    top = tops[0]
    for t in tops[1:]:
        top = jnp.maximum(top, t)
    total = sum(p * jnp.exp(t - top) for p, t in zip(parts, tops))
    row = lax.broadcasted_iota(jnp.int32, total.shape, 0)
    return jnp.where(row == top_row, top, total)


def after(value, *others):
    return lax.optimization_barrier((value, *others))[0]


STEP = 256
LONG = 512
GROUP = 4
WINDOW = 384


def group(j, width, nlat):
    start = GROUP * width * j // 128 * 128
    return slice(start, start + WINDOW), slice(GROUP * nlat * j, GROUP * nlat * (j + 1))


def call(body, steps, ins, outs, scratch, flops, moved, name, room):
    def spec(block, where, buffers):
        if block is None:
            return pl.BlockSpec(memory_space=pl.ANY)
        if where is whole_block and buffers:
            return pl.BlockSpec(block, where, pipeline_mode=pl.Buffered(buffers))
        return pl.BlockSpec(block, where)

    return pl.pallas_call(
        body,
        grid=(steps,),
        in_specs=[spec(b, m, 1) for _, b, m in ins],
        out_specs=[spec(b, m, 0) for _, _, b, m in outs],
        out_shape=[jax.ShapeDtypeStruct(s, t) for s, t, _, _ in outs],
        scratch_shapes=scratch,
        compiler_params=pltpu.CompilerParams(vmem_limit_bytes=room * 2**20),
        cost_estimate=pl.CostEstimate(flops=flops, bytes_accessed=moved, transcendentals=0),
        name=name,
    )(*[a for a, _, _ in ins])


def whole_block(i):
    return (0, 0)


def row_block(i):
    return (i, 0)


def col_block(i):
    return (0, i)


def softmax_kernel(
    rows,
    width,
    nlat,
    x_ref,
    gain_ref,
    wk_far,
    wv_far,
    wq_far,
    lat_ref,
    n_ref,
    v_ref,
    e_ref,
    pack_ref,
    sq_far,
    s_all,
    n_all,
    acc_ref,
    state_ref,
    wk_ref,
    wv_ref,
    wq_ref,
    sq_ref,
    wk_sem,
    wv_sem,
    wq_sem,
    sq_sem,
):
    step, steps = pl.program_id(0), pl.num_programs(0) // 2
    at = pl.multiple_of((step % steps) * STEP, STEP)
    here = pl.ds(at, STEP)

    def valid(columns):
        return lax.broadcasted_iota(jnp.int32, (STEP, columns), 0) + at < rows

    wk_copy = pltpu.make_async_copy(wk_far, wk_ref, wk_sem)
    wv_copy = pltpu.make_async_copy(wv_far, wv_ref, wv_sem)
    wq_copy = pltpu.make_async_copy(wq_far, wq_ref, wq_sem)
    sq_copy = pltpu.make_async_copy(sq_ref, sq_far, sq_sem)

    @pl.when(step == 0)
    def _():
        wq_copy.start()
        wk_copy.start()
        wv_copy.start()
        acc_ref[...] = jnp.zeros_like(acc_ref)
        row = lax.broadcasted_iota(jnp.int32, state_ref.shape, 0)
        state_ref[...] = jnp.where(row == 0, -jnp.inf, 0.0)
        wq_copy.wait()
        twice = jnp.concatenate([lat_ref[...], lat_ref[...]], axis=0)
        query = dot(twice, wq_ref[...]).astype(BF16).astype(F32).T
        sq_ref[...] = jnp.zeros_like(sq_ref)
        head_row = lax.broadcasted_iota(jnp.int32, (2 * width, 2 * nlat), 0) // width
        head_col = lax.broadcasted_iota(jnp.int32, (2 * width, 2 * nlat), 1) // nlat
        for t in range(HEADS // 2):
            feat, cols = slice(2 * width * t, 2 * width * (t + 1)), slice(2 * nlat * t, 2 * nlat * (t + 1))
            sq_ref[feat, cols] = jnp.where(head_row == head_col, query[feat, :], 0.0).astype(BF16)
        sq_copy.start()
        wk_copy.wait()

    @pl.when(step < steps)
    def _():
        x = x_ref[...].astype(F32)
        centred = x - jnp.mean(x, axis=-1, keepdims=True)
        rstd = lax.rsqrt(jnp.mean(centred * centred, axis=-1, keepdims=True) + 1e-06)
        normed = centred * rstd * gain_ref[...].astype(F32)[None, :]
        normed = jnp.where(valid(x.shape[1]), normed, 0.0).astype(BF16)
        n_ref[...] = normed
        keys = dot(normed, wk_ref[...]).astype(BF16)
        n_all[here, :] = normed
        for j in range(HEADS // GROUP):
            feat, cols = group(j, width, nlat)
            s = dot(keys[:, feat], sq_ref[feat, cols]) * (1.0 / width**0.5)
            s = jnp.where(valid(s.shape[1]), s, -jnp.inf)
            s_all[here, cols] = s
            state_ref[0:1, cols] = jnp.maximum(
                state_ref[0:1, cols], jnp.max(s, axis=0, keepdims=True)
            )

    @pl.when(step == steps)
    def _():
        wv_copy.wait()

    @pl.when(step >= steps)
    def _():
        values = dot(n_all[here, :], wv_ref[...]).astype(BF16)
        v_ref[...] = values
        for j in range(HEADS // GROUP):
            feat, cols = group(j, width, nlat)
            e = jnp.exp(s_all[here, cols] - state_ref[0:1, cols])
            state_ref[1:2, cols] += jnp.sum(e, axis=0, keepdims=True)
            e = e.astype(BF16)
            e_ref[:, cols] = e
            acc_ref[j] += dot(values[:, feat], e, 0, 0)

    @pl.when(step == 2 * steps - 1)
    def _():
        for j in range(HEADS // GROUP):
            feat, cols = group(j, width, nlat)
            lane = lax.broadcasted_iota(jnp.int32, (width, GROUP * nlat), 1) // nlat
            out = jnp.zeros((width, GROUP * nlat), F32)
            for g in range(GROUP):
                start = (GROUP * j + g) * width - feat.start
                out = out + jnp.where(lane == g, acc_ref[j, start : start + width, :], 0.0)
            pack_ref[:width, cols] = out
        pack_ref[width:, :] = state_ref[...]
        sq_copy.wait()


def grad_kernel(width, nlat, v_ref, sl_ref, e_ref, state_ref, t_ref, d_ref, keep_ref, send_ref):
    @pl.when(pl.program_id(0) == 0)
    def _():
        keep_ref[...] = jnp.zeros_like(keep_ref)
        send_ref[...] = jnp.zeros_like(send_ref)

    for j in range(HEADS // GROUP):
        feat, cols = group(j, width, nlat)
        dprob = dot(v_ref[:, feat], sl_ref[feat, cols])
        grad = e_ref[:, cols].astype(F32) * (dprob - state_ref[0:1, cols]) * state_ref[1:2, cols]
        d_ref[:, cols] = grad.astype(BF16)
    half = keep_ref.shape[0]
    keep_ref[...] += dot(t_ref[:half, :], d_ref[...])
    send_ref[...] += dot(t_ref[half:, :], d_ref[...])


def back_kernel(d_ref, e_ref, qk_ref, qv_ref, state_ref, x_ref, gain_ref, out_ref, scaled_ref):
    @pl.when(pl.program_id(0) == 0)
    def _():
        scaled_ref[...] = (qv_ref[...].astype(F32) * state_ref[2:3, :]).astype(BF16)

    normed_cot = dot(d_ref[...], qk_ref[...], 1, 1) + dot(e_ref[...], scaled_ref[...], 1, 1)
    x = x_ref[...].astype(F32)
    centred = x - jnp.mean(x, axis=-1, keepdims=True)
    rstd = lax.rsqrt(jnp.mean(centred * centred, axis=-1, keepdims=True) + 1e-06)
    xhat = centred * rstd
    dxhat = normed_cot * gain_ref[...].astype(F32)[None, :]
    mean = jnp.mean(dxhat, axis=-1, keepdims=True)
    slope = jnp.mean(dxhat * xhat, axis=-1, keepdims=True)
    out_ref[...] = ((dxhat - mean - xhat * slope) * rstd).astype(BF16)


def split_kernel(keep_ref, got_ref, *outs):
    for k in range(4):
        for n in range(4):
            place = slice((4 * k + n) * CHUNK, (4 * k + n + 1) * CHUNK)
            outs[n][k * CHUNK : (k + 1) * CHUNK, :] = keep_ref[place, :] + got_ref[place, :]


def per_device(patches, latents, gain, w_query, w_key, w_value, w_out, cotangent):
    core = lax.axis_index("c")
    frames, latent_rows = patches[0], latents[0]
    rows, d = frames.shape
    nlat = latent_rows.shape[0]
    width = d // HEADS
    scale = 1.0 / width**0.5
    cols = HEADS * nlat
    steps = -(-rows // STEP)
    padded = steps * STEP
    half_rows = 16 * CHUNK

    def own_half(value):
        return lax.dynamic_slice_in_dim(value, core * (cols // 2), cols // 2, 1)

    def whole(half, other):
        return jnp.where(
            core == 0, jnp.concatenate([half, other], 1), jnp.concatenate([other, half], 1)
        )

    lc = by_head(dot(w_out, cotangent[0], 1, 1), width)
    lc = own_half(lc + shift(lc, "c", 1))

    frames_1 = after(frames, lc)
    lc_y = [shift(lc, "y", k) for k in (1, 2, 3)]

    def first(i):
        return (jnp.minimum(i, steps - 1), 0)

    def second(i):
        return (jnp.maximum(i - steps, 0), 0)

    normed, values, expo, pack, spread_q = call(
        functools.partial(softmax_kernel, rows, width, nlat),
        2 * steps,
        [
            (frames_1, (STEP, d), first),
            (gain, (d,), lambda i: (0,)),
            (w_key, None, None),
            (w_value, None, None),
            (w_query, None, None),
            (latent_rows, (nlat, d), whole_block),
        ],
        [
            ((padded, d), BF16, (STEP, d), first),
            ((padded, d), BF16, (STEP, d), second),
            ((padded, cols), BF16, (STEP, cols), second),
            ((width + 8, cols), F32, (width + 8, cols), whole_block),
            ((d, cols), BF16, None, None),
        ],
        [
            pltpu.VMEM((padded, cols), F32),
            pltpu.VMEM((padded, d), BF16),
            pltpu.VMEM((HEADS // GROUP, WINDOW, GROUP * nlat), F32),
            pltpu.VMEM((8, cols), F32),
            pltpu.VMEM((d, d), BF16),
            pltpu.VMEM((d, d), BF16),
            pltpu.VMEM((d, d), BF16),
            pltpu.VMEM((d, cols), BF16),
            pltpu.SemaphoreType.DMA,
            pltpu.SemaphoreType.DMA,
            pltpu.SemaphoreType.DMA,
            pltpu.SemaphoreType.DMA,
        ],
        4 * padded * (d * d + WINDOW * cols),
        6 * padded * d + 2 * padded * cols + 2 * d * (2 * d + cols),
        "softmax",
        56,
    )
    lc = sum(lc_y, after(lc, pack))
    pack = after(pack, lc)
    paired = shift(pack, "c", 1)
    top, top_pair = pack[width : width + 1], paired[width : width + 1]
    top2 = jnp.maximum(top, top_pair)
    half = own_half(merge([pack, paired], width))

    turned = dot(chosen_rows(d), after(normed, half), 1, 1).astype(BF16)
    half = jnp.concatenate([half, jnp.tile(top2.reshape(2, cols // 2), (4, 1)), lc], axis=0)
    halves = [half] + [shift(half, "x", k) for k in (1, 2, 3)]
    tops = [h[width + 8 : width + 10].reshape(1, cols) for h in halves]
    top3 = jnp.maximum(jnp.maximum(tops[0], tops[1]), jnp.maximum(tops[2], tops[3]))
    q_key = dot(after(w_key, turned), spread_q).astype(BF16)
    halves[0] = after(halves[0], q_key)
    half = merge([h[: width + 8] for h in halves], width)
    lc = sum(h[width + 16 :] for h in halves)
    lc = whole(lc, shift(lc, "c", 1))
    spread_lc = spread(lc, width)

    half_y = [shift(half, "y", k) for k in (1, 2, 3)]
    u_send = dot(turned[half_rows:], after(expo, half))
    u_got = shift(u_send, "c", 1)
    u = dot(turned[:half_rows], after(expo, u_send))
    half = merge([after(half, u, spread_lc)] + half_y, width)
    pack = whole(half, shift(half, "c", 1))
    gtop, gtotal = pack[width : width + 1], pack[width + 1 : width + 2]
    attn = pack[:width] / gtotal
    factor = jnp.exp(top - gtop) / gtotal
    drift = jnp.sum(lc * attn, axis=0, keepdims=True)
    state = jnp.concatenate([drift, factor * scale, factor, jnp.zeros((5, cols), F32)], axis=0)

    dscore, w, w_send = call(
        functools.partial(grad_kernel, width, nlat),
        padded // LONG,
        [
            (values, (LONG, d), row_block),
            (spread_lc, (d, cols), whole_block),
            (expo, (LONG, cols), row_block),
            (state, (8, cols), whole_block),
            (turned, (2 * half_rows, LONG), col_block),
        ],
        [
            ((padded, cols), BF16, (LONG, cols), row_block),
            ((half_rows, cols), F32, (half_rows, cols), whole_block),
            ((half_rows, cols), F32, (half_rows, cols), whole_block),
        ],
        [],
        2 * padded * cols * (WINDOW + 2 * half_rows),
        2 * padded * (2 * d + 2 * cols) + 12 * half_rows * cols,
        "gradient",
        32,
    )
    w_got = shift(w_send, "c", 1)
    u = after(u, w_send) * jnp.exp(top - top2) + u_got * jnp.exp(top_pair - top2)
    u = u.reshape(4, 4, CHUNK, cols)
    u_x = [shift(u[k], "x", k) for k in (1, 2, 3)]
    cut = jax.ShapeDtypeStruct((4 * CHUNK, cols), F32)
    parts = pl.pallas_call(
        split_kernel,
        out_shape=[cut] * 4,
        compiler_params=pltpu.CompilerParams(vmem_limit_bytes=16 * 2**20),
        cost_estimate=pl.CostEstimate(
            flops=half_rows * cols, bytes_accessed=12 * half_rows * cols, transcendentals=0
        ),
        name="split",
    )(w, w_got)


    q_value = dot(after(w_value, parts[0]), spread_lc).astype(BF16)
    patch_grad = call(
        back_kernel,
        steps,
        [
            (after(dscore, parts[0]), (STEP, cols), row_block),
            (expo, (STEP, cols), row_block),
            (q_key, (d, cols), whole_block),
            (q_value, (d, cols), whole_block),
            (state, (8, cols), whole_block),
            (frames, (STEP, d), row_block),
            (gain, (d,), lambda i: (0,)),
        ],
        [((rows, d), BF16, (STEP, d), row_block)],
        [pltpu.VMEM((d, cols), BF16)],
        4 * padded * d * cols,
        4 * padded * (d + cols) + 4 * d * cols,
        "back",
        28,
    )[0]
    attn_rows = attn.reshape(width, HEADS, nlat).transpose(1, 0, 2).reshape(d, nlat).astype(BF16)
    attended = dot(attn_rows, w_out, 0, 0).astype(BF16)

    u = after(u[0], patch_grad) * jnp.exp(tops[0] - top3) + sum(
        u_x[k - 1] * jnp.exp(tops[k] - top3) for k in (1, 2, 3)
    )
    u = u * (jnp.exp(top3 - gtop) / gtotal)
    w = after(parts[0], patch_grad)
    w = w + shift(parts[1], "y", 1) + shift(parts[2], "y", 2) + shift(parts[3], "y", 3)
    w = w.reshape(4, CHUNK, cols)
    w = w[0] + shift(w[1], "x", 1) + shift(w[2], "x", 2) + shift(w[3], "x", 3)
    u = u[0] + shift(u[1], "y", 1) + shift(u[2], "y", 2) + shift(u[3], "y", 3)
    kv = jnp.concatenate(
        [dot(w.astype(BF16), spread_q, 1, 1), dot(u.astype(BF16), spread_lc, 1, 1)], axis=1
    )
    kv = [kv[k * BLOCK : (k + 1) * BLOCK] for k in range(4)]
    kv_grad = kv[0] + shift(kv[1], "v", 1) + shift(kv[2], "v", 2) + shift(kv[3], "v", 3)
    return (attended[None], patch_grad[None], kv_grad)


def solution(mesh):
    grid = Mesh(mesh.devices.reshape(4, 4, 4, 2), ("v", "y", "x", "c"))
    frame = ("y", "x", "c")
    return jax.shard_map(
        per_device,
        mesh=grid,
        in_specs=(
            P("v", frame, None),
            P("v", None, None),
            P(),
            P(),
            P(),
            P(),
            P(None, frame),
            P("v", None, frame),
        ),
        out_specs=(
            P("v", None, frame),
            P("v", frame, None),
            P(("v", "y", "x", "c"), None),
        ),
        check_vma=False,
    )
```

```python
import functools

import jax
import jax.numpy as jnp
from jax import lax
from jax.experimental import pallas as pl
from jax.experimental.pallas import tpu as pltpu
from jax.sharding import Mesh, PartitionSpec as P

HEADS = 16
BLOCK = 9
CHUNK = 40
F32, BF16 = jnp.float32, jnp.bfloat16


def dot(a, b, ca=1, cb=0):
    return lax.dot_general(a, b, (((ca,), (cb,)), ((), ())), preferred_element_type=F32)


def shift(value, axis, step):
    n = lax.axis_size(axis)
    return lax.ppermute(value, axis, [(i, (i + step) % n) for i in range(n)])


def spread(part, width):
    columns = part.shape[1]
    nlat = columns // HEADS
    row = lax.broadcasted_iota(jnp.int32, (HEADS * width, columns), 0) // width
    col = lax.broadcasted_iota(jnp.int32, (HEADS * width, columns), 1) // nlat
    return jnp.where(row == col, jnp.tile(part, (HEADS, 1)), 0.0).astype(BF16)


def by_head(flat, width):
    nlat = flat.shape[1]
    return flat.reshape(HEADS, width, nlat).transpose(1, 0, 2).reshape(width, HEADS * nlat)


def chosen_rows(d):
    v, y, x, c = (lax.axis_index(a) for a in ("v", "y", "x", "c"))
    at = lax.broadcasted_iota(jnp.int32, (32 * CHUNK, 1), 0)
    place, inner = at // CHUNK, at % CHUNK
    dv, i = inner // BLOCK, inner % BLOCK
    dc, dx, dy = place // 16, (place // 4) % 4, place % 4
    owner = ((((v + dv) % 4) * 4 + (y + dy) % 4) * 4 + (x + dx) % 4) * 2 + (c + dc) % 2
    row = jnp.where(inner < 4 * BLOCK, owner * BLOCK + i, -1)
    return (row == lax.broadcasted_iota(jnp.int32, (32 * CHUNK, d), 1)).astype(BF16)


def merge(parts, top_row):
    tops = [p[top_row : top_row + 1] for p in parts]
    top = tops[0]
    for t in tops[1:]:
        top = jnp.maximum(top, t)
    total = sum(p * jnp.exp(t - top) for p, t in zip(parts, tops))
    row = lax.broadcasted_iota(jnp.int32, total.shape, 0)
    return jnp.where(row == top_row, top, total)


def after(value, *others):
    return lax.optimization_barrier((value, *others))[0]


STEP = 256
LONG = 512
GROUP = 4
WINDOW = 384


def group(j, width, nlat):
    start = GROUP * width * j // 128 * 128
    return slice(start, start + WINDOW), slice(GROUP * nlat * j, GROUP * nlat * (j + 1))


def call(body, steps, ins, outs, scratch, flops, moved, name, room):
    def spec(block, where, buffers):
        if block is None:
            return pl.BlockSpec(memory_space=pl.ANY)
        if where is whole_block and buffers:
            return pl.BlockSpec(block, where, pipeline_mode=pl.Buffered(buffers))
        return pl.BlockSpec(block, where)

    return pl.pallas_call(
        body,
        grid=(steps,),
        in_specs=[spec(b, m, 1) for _, b, m in ins],
        out_specs=[spec(b, m, 0) for _, _, b, m in outs],
        out_shape=[jax.ShapeDtypeStruct(s, t) for s, t, _, _ in outs],
        scratch_shapes=scratch,
        compiler_params=pltpu.CompilerParams(vmem_limit_bytes=room * 2**20),
        cost_estimate=pl.CostEstimate(flops=flops, bytes_accessed=moved, transcendentals=0),
        name=name,
    )(*[a for a, _, _ in ins])


def whole_block(i):
    return (0, 0)


def row_block(i):
    return (i, 0)


def col_block(i):
    return (0, i)


def softmax_kernel(
    rows,
    width,
    nlat,
    x_ref,
    gain_ref,
    wk_far,
    wv_far,
    wq_far,
    lat_ref,
    n_ref,
    v_ref,
    e_ref,
    pack_ref,
    sq_far,
    s_all,
    n_all,
    acc_ref,
    state_ref,
    wk_ref,
    wv_ref,
    wq_ref,
    sq_ref,
    wk_sem,
    wv_sem,
    wq_sem,
    sq_sem,
):
    step, steps = pl.program_id(0), pl.num_programs(0) // 2
    at = pl.multiple_of((step % steps) * STEP, STEP)
    here = pl.ds(at, STEP)

    def valid(columns):
        return lax.broadcasted_iota(jnp.int32, (STEP, columns), 0) + at < rows

    wk_copy = pltpu.make_async_copy(wk_far, wk_ref, wk_sem)
    wv_copy = pltpu.make_async_copy(wv_far, wv_ref, wv_sem)
    wq_copy = pltpu.make_async_copy(wq_far, wq_ref, wq_sem)
    sq_copy = pltpu.make_async_copy(sq_ref, sq_far, sq_sem)

    @pl.when(step == 0)
    def _():
        wq_copy.start()
        wk_copy.start()
        wv_copy.start()
        acc_ref[...] = jnp.zeros_like(acc_ref)
        row = lax.broadcasted_iota(jnp.int32, state_ref.shape, 0)
        state_ref[...] = jnp.where(row == 0, -jnp.inf, 0.0)
        wq_copy.wait()
        twice = jnp.concatenate([lat_ref[...], lat_ref[...]], axis=0)
        query = dot(twice, wq_ref[...]).astype(BF16).astype(F32).T
        sq_ref[...] = jnp.zeros_like(sq_ref)
        head_row = lax.broadcasted_iota(jnp.int32, (2 * width, 2 * nlat), 0) // width
        head_col = lax.broadcasted_iota(jnp.int32, (2 * width, 2 * nlat), 1) // nlat
        for t in range(HEADS // 2):
            feat, cols = slice(2 * width * t, 2 * width * (t + 1)), slice(2 * nlat * t, 2 * nlat * (t + 1))
            sq_ref[feat, cols] = jnp.where(head_row == head_col, query[feat, :], 0.0).astype(BF16)
        sq_copy.start()
        wk_copy.wait()

    @pl.when(step < steps)
    def _():
        x = x_ref[...].astype(F32)
        centred = x - jnp.mean(x, axis=-1, keepdims=True)
        rstd = lax.rsqrt(jnp.mean(centred * centred, axis=-1, keepdims=True) + 1e-06)
        normed = centred * rstd * gain_ref[...].astype(F32)[None, :]
        normed = jnp.where(valid(x.shape[1]), normed, 0.0).astype(BF16)
        n_ref[...] = normed
        keys = dot(normed, wk_ref[...]).astype(BF16)
        unused = jnp.where(valid(1), 0.0, -jnp.inf)
        n_all[here, :] = normed
        for j in range(HEADS // GROUP):
            feat, cols = group(j, width, nlat)
            s = dot(keys[:, feat], sq_ref[feat, cols]) * (1.0 / width**0.5) + unused
            s_all[here, cols] = s
            state_ref[0:1, cols] = jnp.maximum(
                state_ref[0:1, cols], jnp.max(s, axis=0, keepdims=True)
            )

    @pl.when(step == steps)
    def _():
        wv_copy.wait()

    @pl.when(step >= steps)
    def _():
        values = dot(n_all[here, :], wv_ref[...]).astype(BF16)
        v_ref[...] = values
        for j in range(HEADS // GROUP):
            feat, cols = group(j, width, nlat)
            e = jnp.exp(s_all[here, cols] - state_ref[0:1, cols])
            state_ref[1:2, cols] += jnp.sum(e, axis=0, keepdims=True)
            e = e.astype(BF16)
            e_ref[:, cols] = e
            acc_ref[j] += dot(values[:, feat], e, 0, 0)

    @pl.when(step == 2 * steps - 1)
    def _():
        for j in range(HEADS // GROUP):
            feat, cols = group(j, width, nlat)
            lane = lax.broadcasted_iota(jnp.int32, (width, GROUP * nlat), 1) // nlat
            out = jnp.zeros((width, GROUP * nlat), F32)
            for g in range(GROUP):
                start = (GROUP * j + g) * width - feat.start
                out = out + jnp.where(lane == g, acc_ref[j, start : start + width, :], 0.0)
            pack_ref[:width, cols] = out
        pack_ref[width:, :] = state_ref[...]
        sq_copy.wait()


def grad_kernel(width, nlat, v_ref, sl_ref, e_ref, state_ref, t_ref, d_ref, keep_ref, send_ref):
    @pl.when(pl.program_id(0) == 0)
    def _():
        keep_ref[...] = jnp.zeros_like(keep_ref)
        send_ref[...] = jnp.zeros_like(send_ref)

    for j in range(HEADS // GROUP):
        feat, cols = group(j, width, nlat)
        dprob = dot(v_ref[:, feat], sl_ref[feat, cols])
        grad = e_ref[:, cols].astype(F32) * (dprob - state_ref[0:1, cols]) * state_ref[1:2, cols]
        d_ref[:, cols] = grad.astype(BF16)
    half = keep_ref.shape[0]
    keep_ref[...] += dot(t_ref[:half, :], d_ref[...])
    send_ref[...] += dot(t_ref[half:, :], d_ref[...])


def back_kernel(d_ref, e_ref, qk_ref, qv_ref, state_ref, x_ref, gain_ref, out_ref, scaled_ref):
    @pl.when(pl.program_id(0) == 0)
    def _():
        scaled_ref[...] = (qv_ref[...].astype(F32) * state_ref[2:3, :]).astype(BF16)

    normed_cot = dot(d_ref[...], qk_ref[...], 1, 1) + dot(e_ref[...], scaled_ref[...], 1, 1)
    x = x_ref[...].astype(F32)
    centred = x - jnp.mean(x, axis=-1, keepdims=True)
    rstd = lax.rsqrt(jnp.mean(centred * centred, axis=-1, keepdims=True) + 1e-06)
    xhat = centred * rstd
    dxhat = normed_cot * gain_ref[...].astype(F32)[None, :]
    mean = jnp.mean(dxhat, axis=-1, keepdims=True)
    slope = jnp.mean(dxhat * xhat, axis=-1, keepdims=True)
    out_ref[...] = ((dxhat - mean - xhat * slope) * rstd).astype(BF16)


def pair_kernel(width, core_ref, own_ref, got_ref, lc_ref, out_ref):
    cut = out_ref.shape[1]
    top = jnp.maximum(own_ref[width : width + 1, :], got_ref[width : width + 1, :])
    here = pl.ds(pl.multiple_of(core_ref[0] * cut, cut), cut)
    own, got = own_ref[:, here], got_ref[:, here]
    own_top, got_top = own[width : width + 1, :], got[width : width + 1, :]
    best = jnp.maximum(own_top, got_top)
    both = own * jnp.exp(own_top - best) + got * jnp.exp(got_top - best)
    row = lax.broadcasted_iota(jnp.int32, both.shape, 0)
    out_ref[: width + 8, :] = jnp.where(row == width, best, both)
    row = lax.broadcasted_iota(jnp.int32, (8, cut), 0)
    out_ref[width + 8 : width + 16, :] = jnp.where(row % 2 == 0, top[:, :cut], top[:, cut:])
    out_ref[width + 16 :, :] = lc_ref[...]


def split_kernel(keep_ref, got_ref, *outs):
    for k in range(4):
        for n in range(4):
            place = slice((4 * k + n) * CHUNK, (4 * k + n + 1) * CHUNK)
            outs[n][k * CHUNK : (k + 1) * CHUNK, :] = keep_ref[place, :] + got_ref[place, :]


def per_device(patches, latents, gain, w_query, w_key, w_value, w_out, cotangent):
    core = lax.axis_index("c")
    frames, latent_rows = patches[0], latents[0]
    rows, d = frames.shape
    nlat = latent_rows.shape[0]
    width = d // HEADS
    scale = 1.0 / width**0.5
    cols = HEADS * nlat
    steps = -(-rows // STEP)
    padded = steps * STEP
    half_rows = 16 * CHUNK

    def own_half(value):
        return lax.dynamic_slice_in_dim(value, core * (cols // 2), cols // 2, 1)

    def whole(half, other):
        return jnp.where(
            core == 0, jnp.concatenate([half, other], 1), jnp.concatenate([other, half], 1)
        )

    lc = by_head(dot(w_out, cotangent[0], 1, 1), width)
    lc = own_half(lc + shift(lc, "c", 1))

    frames_1 = after(frames, lc)
    lc_y = [shift(lc, "y", k) for k in (1, 2, 3)]

    def first(i):
        return (jnp.minimum(i, steps - 1), 0)

    def second(i):
        return (jnp.maximum(i - steps, 0), 0)

    normed, values, expo, pack, spread_q = call(
        functools.partial(softmax_kernel, rows, width, nlat),
        2 * steps,
        [
            (frames_1, (STEP, d), first),
            (gain, (d,), lambda i: (0,)),
            (w_key, None, None),
            (w_value, None, None),
            (w_query, None, None),
            (latent_rows, (nlat, d), whole_block),
        ],
        [
            ((padded, d), BF16, (STEP, d), first),
            ((padded, d), BF16, (STEP, d), second),
            ((padded, cols), BF16, (STEP, cols), second),
            ((width + 8, cols), F32, (width + 8, cols), whole_block),
            ((d, cols), BF16, None, None),
        ],
        [
            pltpu.VMEM((padded, cols), F32),
            pltpu.VMEM((padded, d), BF16),
            pltpu.VMEM((HEADS // GROUP, WINDOW, GROUP * nlat), F32),
            pltpu.VMEM((8, cols), F32),
            pltpu.VMEM((d, d), BF16),
            pltpu.VMEM((d, d), BF16),
            pltpu.VMEM((d, d), BF16),
            pltpu.VMEM((d, cols), BF16),
            pltpu.SemaphoreType.DMA,
            pltpu.SemaphoreType.DMA,
            pltpu.SemaphoreType.DMA,
            pltpu.SemaphoreType.DMA,
        ],
        4 * padded * (d * d + WINDOW * cols),
        6 * padded * d + 2 * padded * cols + 2 * d * (2 * d + cols),
        "softmax",
        56,
    )
    lc = sum(lc_y, after(lc, pack))
    pack = after(pack, lc)
    paired = shift(pack, "c", 1)
    top, top_pair = pack[width : width + 1], paired[width : width + 1]
    top2 = jnp.maximum(top, top_pair)
    vmem = pl.BlockSpec(memory_space=pltpu.VMEM)
    half = pl.pallas_call(
        functools.partial(pair_kernel, width),
        in_specs=[pl.BlockSpec(memory_space=pltpu.SMEM), vmem, vmem, vmem],
        out_specs=vmem,
        out_shape=jax.ShapeDtypeStruct((2 * width + 16, cols // 2), F32),
        compiler_params=pltpu.CompilerParams(vmem_limit_bytes=16 * 2**20),
        name="pair",
    )(core.astype(jnp.int32).reshape(1), pack, paired, lc)

    turned = dot(chosen_rows(d), after(normed, half), 1, 1).astype(BF16)
    halves = [half] + [shift(half, "x", k) for k in (1, 2, 3)]
    tops = [h[width + 8 : width + 10].reshape(1, cols) for h in halves]
    top3 = jnp.maximum(jnp.maximum(tops[0], tops[1]), jnp.maximum(tops[2], tops[3]))
    q_key = dot(after(w_key, turned), spread_q).astype(BF16)
    halves[0] = after(halves[0], q_key)
    half = merge([h[: width + 8] for h in halves], width)
    lc = sum(h[width + 16 :] for h in halves)
    lc = whole(lc, shift(lc, "c", 1))
    spread_lc = spread(lc, width)

    half_y = [shift(half, "y", k) for k in (1, 2, 3)]
    u_send = dot(turned[half_rows:], after(expo, half))
    u_got = shift(u_send, "c", 1)
    u = dot(turned[:half_rows], after(expo, u_send))
    half = merge([after(half, u, spread_lc)] + half_y, width)
    pack = whole(half, shift(half, "c", 1))
    gtop, gtotal = pack[width : width + 1], pack[width + 1 : width + 2]
    attn = pack[:width] / gtotal
    factor = jnp.exp(top - gtop) / gtotal
    drift = jnp.sum(lc * attn, axis=0, keepdims=True)
    state = jnp.concatenate([drift, factor * scale, factor, jnp.zeros((5, cols), F32)], axis=0)

    dscore, w, w_send = call(
        functools.partial(grad_kernel, width, nlat),
        padded // LONG,
        [
            (values, (LONG, d), row_block),
            (spread_lc, (d, cols), whole_block),
            (expo, (LONG, cols), row_block),
            (state, (8, cols), whole_block),
            (turned, (2 * half_rows, LONG), col_block),
        ],
        [
            ((padded, cols), BF16, (LONG, cols), row_block),
            ((half_rows, cols), F32, (half_rows, cols), whole_block),
            ((half_rows, cols), F32, (half_rows, cols), whole_block),
        ],
        [],
        2 * padded * cols * (WINDOW + 2 * half_rows),
        2 * padded * (2 * d + 2 * cols) + 12 * half_rows * cols,
        "gradient",
        32,
    )
    w_got = shift(w_send, "c", 1)
    u = after(u, w_send) * jnp.exp(top - top2) + u_got * jnp.exp(top_pair - top2)
    u = u.reshape(4, 4, CHUNK, cols)
    u_x = [shift(u[k], "x", k) for k in (1, 2, 3)]
    cut = jax.ShapeDtypeStruct((4 * CHUNK, cols), F32)
    parts = pl.pallas_call(
        split_kernel,
        out_shape=[cut] * 4,
        compiler_params=pltpu.CompilerParams(vmem_limit_bytes=16 * 2**20),
        cost_estimate=pl.CostEstimate(
            flops=half_rows * cols, bytes_accessed=12 * half_rows * cols, transcendentals=0
        ),
        name="split",
    )(w, w_got)


    q_value = dot(after(w_value, parts[0]), spread_lc).astype(BF16)
    patch_grad = call(
        back_kernel,
        steps,
        [
            (after(dscore, parts[0]), (STEP, cols), row_block),
            (expo, (STEP, cols), row_block),
            (q_key, (d, cols), whole_block),
            (q_value, (d, cols), whole_block),
            (state, (8, cols), whole_block),
            (frames, (STEP, d), row_block),
            (gain, (d,), lambda i: (0,)),
        ],
        [((rows, d), BF16, (STEP, d), row_block)],
        [pltpu.VMEM((d, cols), BF16)],
        4 * padded * d * cols,
        4 * padded * (d + cols) + 4 * d * cols,
        "back",
        28,
    )[0]
    attn_rows = attn.reshape(width, HEADS, nlat).transpose(1, 0, 2).reshape(d, nlat).astype(BF16)
    attended = dot(attn_rows, w_out, 0, 0).astype(BF16)

    u = after(u[0], patch_grad) * jnp.exp(tops[0] - top3) + sum(
        u_x[k - 1] * jnp.exp(tops[k] - top3) for k in (1, 2, 3)
    )
    u = u * (jnp.exp(top3 - gtop) / gtotal)
    w = after(parts[0], patch_grad)
    w = w + shift(parts[1], "y", 1) + shift(parts[2], "y", 2) + shift(parts[3], "y", 3)
    w = w.reshape(4, CHUNK, cols)
    w = w[0] + shift(w[1], "x", 1) + shift(w[2], "x", 2) + shift(w[3], "x", 3)
    u = u[0] + shift(u[1], "y", 1) + shift(u[2], "y", 2) + shift(u[3], "y", 3)
    kv = jnp.concatenate(
        [dot(w.astype(BF16), spread_q, 1, 1), dot(u.astype(BF16), spread_lc, 1, 1)], axis=1
    )
    kv = [kv[k * BLOCK : (k + 1) * BLOCK] for k in range(4)]
    kv_grad = kv[0] + shift(kv[1], "v", 1) + shift(kv[2], "v", 2) + shift(kv[3], "v", 3)
    return (attended[None], patch_grad[None], kv_grad)


def solution(mesh):
    grid = Mesh(mesh.devices.reshape(4, 4, 4, 2), ("v", "y", "x", "c"))
    frame = ("y", "x", "c")
    return jax.shard_map(
        per_device,
        mesh=grid,
        in_specs=(
            P("v", frame, None),
            P("v", None, None),
            P(),
            P(),
            P(),
            P(),
            P(None, frame),
            P("v", None, frame),
        ),
        out_specs=(
            P("v", None, frame),
            P("v", frame, None),
            P(("v", "y", "x", "c"), None),
        ),
        check_vma=False,
    )
```

```python
import functools

import jax
import jax.numpy as jnp
from jax import lax
from jax.experimental import pallas as pl
from jax.experimental.pallas import tpu as pltpu
from jax.sharding import Mesh, PartitionSpec as P

HEADS = 16
BLOCK = 9
CHUNK = 40
F32, BF16 = jnp.float32, jnp.bfloat16


def dot(a, b, ca=1, cb=0):
    return lax.dot_general(a, b, (((ca,), (cb,)), ((), ())), preferred_element_type=F32)


def shift(value, axis, step):
    n = lax.axis_size(axis)
    return lax.ppermute(value, axis, [(i, (i + step) % n) for i in range(n)])


def spread(part, width):
    columns = part.shape[1]
    nlat = columns // HEADS
    row = lax.broadcasted_iota(jnp.int32, (HEADS * width, columns), 0) // width
    col = lax.broadcasted_iota(jnp.int32, (HEADS * width, columns), 1) // nlat
    return jnp.where(row == col, jnp.tile(part, (HEADS, 1)), 0.0).astype(BF16)


def by_head(flat, width):
    nlat = flat.shape[1]
    return flat.reshape(HEADS, width, nlat).transpose(1, 0, 2).reshape(width, HEADS * nlat)


def chosen_rows(d):
    v, y, x, c = (lax.axis_index(a) for a in ("v", "y", "x", "c"))
    at = lax.broadcasted_iota(jnp.int32, (32 * CHUNK, 1), 0)
    place, inner = at // CHUNK, at % CHUNK
    dv, i = inner // BLOCK, inner % BLOCK
    dc, dx, dy = place // 16, (place // 4) % 4, place % 4
    owner = ((((v + dv) % 4) * 4 + (y + dy) % 4) * 4 + (x + dx) % 4) * 2 + (c + dc) % 2
    row = jnp.where(inner < 4 * BLOCK, owner * BLOCK + i, -1)
    return (row == lax.broadcasted_iota(jnp.int32, (32 * CHUNK, d), 1)).astype(BF16)


def merge(parts, top_row):
    tops = [p[top_row : top_row + 1] for p in parts]
    top = tops[0]
    for t in tops[1:]:
        top = jnp.maximum(top, t)
    total = sum(p * jnp.exp(t - top) for p, t in zip(parts, tops))
    row = lax.broadcasted_iota(jnp.int32, total.shape, 0)
    return jnp.where(row == top_row, top, total)


def after(value, *others):
    return lax.optimization_barrier((value, *others))[0]


STEP = 256
LONG = 512
GROUP = 4
WINDOW = 384


def group(j, width, nlat):
    start = GROUP * width * j // 128 * 128
    return slice(start, start + WINDOW), slice(GROUP * nlat * j, GROUP * nlat * (j + 1))


def call(body, steps, ins, outs, scratch, flops, moved, name, room):
    def spec(block, where, buffers):
        if block is None:
            return pl.BlockSpec(memory_space=pl.ANY)
        if where is whole_block and buffers:
            return pl.BlockSpec(block, where, pipeline_mode=pl.Buffered(buffers))
        return pl.BlockSpec(block, where)

    return pl.pallas_call(
        body,
        grid=(steps,),
        in_specs=[spec(b, m, 1) for _, b, m in ins],
        out_specs=[spec(b, m, 0) for _, _, b, m in outs],
        out_shape=[jax.ShapeDtypeStruct(s, t) for s, t, _, _ in outs],
        scratch_shapes=scratch,
        compiler_params=pltpu.CompilerParams(vmem_limit_bytes=room * 2**20),
        cost_estimate=pl.CostEstimate(flops=flops, bytes_accessed=moved, transcendentals=0),
        name=name,
    )(*[a for a, _, _ in ins])


def whole_block(i):
    return (0, 0)


def row_block(i):
    return (i, 0)


def col_block(i):
    return (0, i)


def softmax_kernel(
    rows,
    width,
    nlat,
    x_ref,
    gain_ref,
    wk_far,
    wv_far,
    wq_far,
    lat_ref,
    n_ref,
    v_ref,
    e_ref,
    pack_ref,
    sq_far,
    s_all,
    n_all,
    acc_ref,
    state_ref,
    wk_ref,
    wv_ref,
    wq_ref,
    sq_ref,
    wk_sem,
    wv_sem,
    wq_sem,
    sq_sem,
):
    step, steps = pl.program_id(0), pl.num_programs(0) // 2
    at = pl.multiple_of((step % steps) * STEP, STEP)
    here = pl.ds(at, STEP)

    def valid(columns):
        return lax.broadcasted_iota(jnp.int32, (STEP, columns), 0) + at < rows

    wk_copy = pltpu.make_async_copy(wk_far, wk_ref, wk_sem)
    wv_copy = pltpu.make_async_copy(wv_far, wv_ref, wv_sem)
    wq_copy = pltpu.make_async_copy(wq_far, wq_ref, wq_sem)
    sq_copy = pltpu.make_async_copy(sq_ref, sq_far, sq_sem)

    @pl.when(step == 0)
    def _():
        wq_copy.start()
        wk_copy.start()
        wv_copy.start()
        acc_ref[...] = jnp.zeros_like(acc_ref)
        row = lax.broadcasted_iota(jnp.int32, state_ref.shape, 0)
        state_ref[...] = jnp.where(row == 0, -jnp.inf, 0.0)
        wq_copy.wait()
        twice = jnp.concatenate([lat_ref[...], lat_ref[...]], axis=0)
        query = dot(twice, wq_ref[...]).astype(BF16).astype(F32).T
        sq_ref[...] = jnp.zeros_like(sq_ref)
        head_row = lax.broadcasted_iota(jnp.int32, (2 * width, 2 * nlat), 0) // width
        head_col = lax.broadcasted_iota(jnp.int32, (2 * width, 2 * nlat), 1) // nlat
        for t in range(HEADS // 2):
            feat, cols = slice(2 * width * t, 2 * width * (t + 1)), slice(2 * nlat * t, 2 * nlat * (t + 1))
            sq_ref[feat, cols] = jnp.where(head_row == head_col, query[feat, :], 0.0).astype(BF16)
        sq_copy.start()
        wk_copy.wait()

    @pl.when(step < steps)
    def _():
        x = x_ref[...].astype(F32)
        centred = x - jnp.mean(x, axis=-1, keepdims=True)
        rstd = lax.rsqrt(jnp.mean(centred * centred, axis=-1, keepdims=True) + 1e-06)
        normed = centred * rstd * gain_ref[...].astype(F32)[None, :]
        normed = jnp.where(valid(x.shape[1]), normed, 0.0).astype(BF16)
        n_ref[...] = normed
        keys = dot(normed, wk_ref[...]).astype(BF16)
        unused = jnp.where(valid(1), 0.0, -jnp.inf)
        n_all[here, :] = normed
        for j in range(HEADS // GROUP):
            feat, cols = group(j, width, nlat)
            s = dot(keys[:, feat], sq_ref[feat, cols]) * (1.0 / width**0.5) + unused
            s_all[here, cols] = s
            state_ref[0:1, cols] = jnp.maximum(
                state_ref[0:1, cols], jnp.max(s, axis=0, keepdims=True)
            )

    @pl.when(step == steps)
    def _():
        wv_copy.wait()

    @pl.when(step >= steps)
    def _():
        values = dot(n_all[here, :], wv_ref[...]).astype(BF16)
        v_ref[...] = values
        for j in range(HEADS // GROUP):
            feat, cols = group(j, width, nlat)
            e = jnp.exp(s_all[here, cols] - state_ref[0:1, cols])
            state_ref[1:2, cols] += jnp.sum(e, axis=0, keepdims=True)
            e = e.astype(BF16)
            e_ref[:, cols] = e
            acc_ref[j] += dot(values[:, feat], e, 0, 0)

    @pl.when(step == 2 * steps - 1)
    def _():
        for j in range(HEADS // GROUP):
            feat, cols = group(j, width, nlat)
            lane = lax.broadcasted_iota(jnp.int32, (width, GROUP * nlat), 1) // nlat
            out = jnp.zeros((width, GROUP * nlat), F32)
            for g in range(GROUP):
                start = (GROUP * j + g) * width - feat.start
                out = out + jnp.where(lane == g, acc_ref[j, start : start + width, :], 0.0)
            pack_ref[:width, cols] = out
        pack_ref[width:, :] = state_ref[...]
        sq_copy.wait()


def grad_kernel(width, nlat, v_ref, sl_ref, e_ref, state_ref, t_ref, d_ref, keep_ref, send_ref):
    @pl.when(pl.program_id(0) == 0)
    def _():
        keep_ref[...] = jnp.zeros_like(keep_ref)
        send_ref[...] = jnp.zeros_like(send_ref)

    for j in range(HEADS // GROUP):
        feat, cols = group(j, width, nlat)
        dprob = dot(v_ref[:, feat], sl_ref[feat, cols])
        grad = e_ref[:, cols].astype(F32) * (dprob - state_ref[0:1, cols]) * state_ref[1:2, cols]
        d_ref[:, cols] = grad.astype(BF16)
    half = keep_ref.shape[0]
    keep_ref[...] += dot(t_ref[:half, :], d_ref[...])
    send_ref[...] += dot(t_ref[half:, :], d_ref[...])


def back_kernel(d_ref, e_ref, qk_ref, qv_ref, state_ref, x_ref, gain_ref, out_ref, scaled_ref):
    @pl.when(pl.program_id(0) == 0)
    def _():
        scaled_ref[...] = (qv_ref[...].astype(F32) * state_ref[2:3, :]).astype(BF16)

    normed_cot = dot(d_ref[...], qk_ref[...], 1, 1) + dot(e_ref[...], scaled_ref[...], 1, 1)
    x = x_ref[...].astype(F32)
    centred = x - jnp.mean(x, axis=-1, keepdims=True)
    rstd = lax.rsqrt(jnp.mean(centred * centred, axis=-1, keepdims=True) + 1e-06)
    xhat = centred * rstd
    dxhat = normed_cot * gain_ref[...].astype(F32)[None, :]
    mean = jnp.mean(dxhat, axis=-1, keepdims=True)
    slope = jnp.mean(dxhat * xhat, axis=-1, keepdims=True)
    out_ref[...] = ((dxhat - mean - xhat * slope) * rstd).astype(BF16)


def pair_kernel(width, core_ref, own_ref, got_ref, lc_ref, out_ref):
    cut = out_ref.shape[1]
    top = jnp.maximum(own_ref[width : width + 1, :], got_ref[width : width + 1, :])
    here = pl.ds(pl.multiple_of(core_ref[0] * cut, cut), cut)
    own, got = own_ref[:, here], got_ref[:, here]
    own_top, got_top = own[width : width + 1, :], got[width : width + 1, :]
    best = jnp.maximum(own_top, got_top)
    both = own * jnp.exp(own_top - best) + got * jnp.exp(got_top - best)
    row = lax.broadcasted_iota(jnp.int32, both.shape, 0)
    out_ref[: width + 8, :] = jnp.where(row == width, best, both)
    row = lax.broadcasted_iota(jnp.int32, (8, cut), 0)
    out_ref[width + 8 : width + 16, :] = jnp.where(row % 2 == 0, top[:, :cut], top[:, cut:])
    out_ref[width + 16 :, :] = jnp.zeros((width // 3, cut), F32)
    for b in range(3):
        rows = slice(width // 3 * b, width // 3 * (b + 1))
        out_ref[width + 16 :, 128 * b : 128 * (b + 1)] = lc_ref[rows, :]


def split_kernel(keep_ref, got_ref, *outs):
    for k in range(4):
        for n in range(4):
            place = slice((4 * k + n) * CHUNK, (4 * k + n + 1) * CHUNK)
            outs[n][k * CHUNK : (k + 1) * CHUNK, :] = keep_ref[place, :] + got_ref[place, :]


def per_device(patches, latents, gain, w_query, w_key, w_value, w_out, cotangent):
    core = lax.axis_index("c")
    frames, latent_rows = patches[0], latents[0]
    rows, d = frames.shape
    nlat = latent_rows.shape[0]
    width = d // HEADS
    scale = 1.0 / width**0.5
    cols = HEADS * nlat
    steps = -(-rows // STEP)
    padded = steps * STEP
    half_rows = 16 * CHUNK

    def own_half(value):
        return lax.dynamic_slice_in_dim(value, core * (cols // 2), cols // 2, 1)

    def whole(half, other):
        return jnp.where(
            core == 0, jnp.concatenate([half, other], 1), jnp.concatenate([other, half], 1)
        )

    lc = by_head(dot(w_out, cotangent[0], 1, 1), width)
    lc = own_half(lc + shift(lc, "c", 1))

    frames_1 = after(frames, lc)
    here = lax.axis_index("y")
    part = cols // 8

    def of_row(k):
        return lax.dynamic_slice_in_dim(lc, (here + k) % 4 * part, part, 1)

    lc_y = [shift(of_row(k), "y", k) for k in (1, 2, 3)]
    lc = of_row(0)

    def first(i):
        return (jnp.minimum(i, steps - 1), 0)

    def second(i):
        return (jnp.maximum(i - steps, 0), 0)

    normed, values, expo, pack, spread_q = call(
        functools.partial(softmax_kernel, rows, width, nlat),
        2 * steps,
        [
            (frames_1, (STEP, d), first),
            (gain, (d,), lambda i: (0,)),
            (w_key, None, None),
            (w_value, None, None),
            (w_query, None, None),
            (latent_rows, (nlat, d), whole_block),
        ],
        [
            ((padded, d), BF16, (STEP, d), first),
            ((padded, d), BF16, (STEP, d), second),
            ((padded, cols), BF16, (STEP, cols), second),
            ((width + 8, cols), F32, (width + 8, cols), whole_block),
            ((d, cols), BF16, None, None),
        ],
        [
            pltpu.VMEM((padded, cols), F32),
            pltpu.VMEM((padded, d), BF16),
            pltpu.VMEM((HEADS // GROUP, WINDOW, GROUP * nlat), F32),
            pltpu.VMEM((8, cols), F32),
            pltpu.VMEM((d, d), BF16),
            pltpu.VMEM((d, d), BF16),
            pltpu.VMEM((d, d), BF16),
            pltpu.VMEM((d, cols), BF16),
            pltpu.SemaphoreType.DMA,
            pltpu.SemaphoreType.DMA,
            pltpu.SemaphoreType.DMA,
            pltpu.SemaphoreType.DMA,
        ],
        4 * padded * (d * d + WINDOW * cols),
        6 * padded * d + 2 * padded * cols + 2 * d * (2 * d + cols),
        "softmax",
        56,
    )
    lc = sum(lc_y, after(lc, pack))
    pack = after(pack, lc)
    paired = shift(pack, "c", 1)
    top, top_pair = pack[width : width + 1], paired[width : width + 1]
    top2 = jnp.maximum(top, top_pair)
    vmem = pl.BlockSpec(memory_space=pltpu.VMEM)
    half = pl.pallas_call(
        functools.partial(pair_kernel, width),
        in_specs=[pl.BlockSpec(memory_space=pltpu.SMEM), vmem, vmem, vmem],
        out_specs=vmem,
        out_shape=jax.ShapeDtypeStruct((width + 16 + width // 3, cols // 2), F32),
        compiler_params=pltpu.CompilerParams(vmem_limit_bytes=16 * 2**20),
        name="pair",
    )(core.astype(jnp.int32).reshape(1), pack, paired, lc)

    turned = dot(chosen_rows(d), after(normed, half), 1, 1).astype(BF16)
    halves = [half] + [shift(half, "x", k) for k in (1, 2, 3)]
    tops = [h[width + 8 : width + 10].reshape(1, cols) for h in halves]
    top3 = jnp.maximum(jnp.maximum(tops[0], tops[1]), jnp.maximum(tops[2], tops[3]))
    halves[0] = after(halves[0], turned)
    half = merge([h[: width + 8] for h in halves], width)
    lc = sum(h[width + 16 :] for h in halves)

    half = jnp.concatenate([half, lc], axis=0)
    half_y = [shift(half, "y", k) for k in (1, 2, 3)]
    u_send = dot(turned[half_rows:], after(expo, half))
    u_got = shift(u_send, "c", 1)
    u = dot(turned[:half_rows], after(expo, u_send))
    half_y = [after(half, u)] + half_y
    column = lax.broadcasted_iota(jnp.int32, (width, cols // 2), 1) // part
    lc = jnp.zeros((width, cols // 2), F32)
    for k in range(4):
        got = half_y[k][width + 8 :]
        got = jnp.concatenate([got[:, 128 * b : 128 * (b + 1)] for b in range(3)], axis=0)
        lc = jnp.where(column == (here - k) % 4, jnp.tile(got, (1, 4)), lc)
    half = merge([h[: width + 8] for h in half_y], width)
    half = jnp.concatenate([half, lc], axis=0)
    pack = whole(half, shift(half, "c", 1))
    pack, lc = pack[: width + 8], pack[width + 8 :]
    gtop, gtotal = pack[width : width + 1], pack[width + 1 : width + 2]
    attn = pack[:width] / gtotal
    factor = jnp.exp(top - gtop) / gtotal
    drift = jnp.sum(lc * attn, axis=0, keepdims=True)
    state = jnp.concatenate([drift, factor * scale, factor, jnp.zeros((5, cols), F32)], axis=0)

    spread_lc = spread(lc, width)

    dscore, w, w_send = call(
        functools.partial(grad_kernel, width, nlat),
        padded // LONG,
        [
            (values, (LONG, d), row_block),
            (spread_lc, (d, cols), whole_block),
            (expo, (LONG, cols), row_block),
            (state, (8, cols), whole_block),
            (turned, (2 * half_rows, LONG), col_block),
        ],
        [
            ((padded, cols), BF16, (LONG, cols), row_block),
            ((half_rows, cols), F32, (half_rows, cols), whole_block),
            ((half_rows, cols), F32, (half_rows, cols), whole_block),
        ],
        [],
        2 * padded * cols * (WINDOW + 2 * half_rows),
        2 * padded * (2 * d + 2 * cols) + 12 * half_rows * cols,
        "gradient",
        32,
    )
    w_got = shift(w_send, "c", 1)
    u = after(u, w_send) * jnp.exp(top - top2) + u_got * jnp.exp(top_pair - top2)
    u = u.reshape(4, 4, CHUNK, cols)
    u_x = [shift(u[k], "x", k) for k in (1, 2, 3)]
    cut = jax.ShapeDtypeStruct((4 * CHUNK, cols), F32)
    parts = pl.pallas_call(
        split_kernel,
        out_shape=[cut] * 4,
        compiler_params=pltpu.CompilerParams(vmem_limit_bytes=16 * 2**20),
        cost_estimate=pl.CostEstimate(
            flops=half_rows * cols, bytes_accessed=12 * half_rows * cols, transcendentals=0
        ),
        name="split",
    )(w, w_got)


    q_key = dot(after(w_key, parts[0]), spread_q).astype(BF16)
    q_value = dot(after(w_value, parts[0]), spread_lc).astype(BF16)
    patch_grad = call(
        back_kernel,
        steps,
        [
            (after(dscore, parts[0]), (STEP, cols), row_block),
            (expo, (STEP, cols), row_block),
            (q_key, (d, cols), whole_block),
            (q_value, (d, cols), whole_block),
            (state, (8, cols), whole_block),
            (frames, (STEP, d), row_block),
            (gain, (d,), lambda i: (0,)),
        ],
        [((rows, d), BF16, (STEP, d), row_block)],
        [pltpu.VMEM((d, cols), BF16)],
        4 * padded * d * cols,
        4 * padded * (d + cols) + 4 * d * cols,
        "back",
        28,
    )[0]
    attn_rows = attn.reshape(width, HEADS, nlat).transpose(1, 0, 2).reshape(d, nlat).astype(BF16)
    attended = dot(attn_rows, w_out, 0, 0).astype(BF16)

    u = after(u[0], patch_grad) * jnp.exp(tops[0] - top3) + sum(
        u_x[k - 1] * jnp.exp(tops[k] - top3) for k in (1, 2, 3)
    )
    u = u * (jnp.exp(top3 - gtop) / gtotal)
    w = after(parts[0], patch_grad)
    w = w + shift(parts[1], "y", 1) + shift(parts[2], "y", 2) + shift(parts[3], "y", 3)
    w = w.reshape(4, CHUNK, cols)
    w = w[0] + shift(w[1], "x", 1) + shift(w[2], "x", 2) + shift(w[3], "x", 3)
    u = u[0] + shift(u[1], "y", 1) + shift(u[2], "y", 2) + shift(u[3], "y", 3)
    kv = jnp.concatenate(
        [dot(w.astype(BF16), spread_q, 1, 1), dot(u.astype(BF16), spread_lc, 1, 1)], axis=1
    )
    kv = [kv[k * BLOCK : (k + 1) * BLOCK] for k in range(4)]
    kv_grad = kv[0] + shift(kv[1], "v", 1) + shift(kv[2], "v", 2) + shift(kv[3], "v", 3)
    return (attended[None], patch_grad[None], kv_grad)


def solution(mesh):
    grid = Mesh(mesh.devices.reshape(4, 4, 4, 2), ("v", "y", "x", "c"))
    frame = ("y", "x", "c")
    return jax.shard_map(
        per_device,
        mesh=grid,
        in_specs=(
            P("v", frame, None),
            P("v", None, None),
            P(),
            P(),
            P(),
            P(),
            P(None, frame),
            P("v", None, frame),
        ),
        out_specs=(
            P("v", None, frame),
            P("v", frame, None),
            P(("v", "y", "x", "c"), None),
        ),
        check_vma=False,
    )
```

```python
import functools

import jax
import jax.numpy as jnp
from jax import lax
from jax.experimental import pallas as pl
from jax.experimental.pallas import tpu as pltpu
from jax.sharding import Mesh, PartitionSpec as P

HEADS = 16
BLOCK = 9
CHUNK = 40
F32, BF16 = jnp.float32, jnp.bfloat16


def dot(a, b, ca=1, cb=0):
    return lax.dot_general(a, b, (((ca,), (cb,)), ((), ())), preferred_element_type=F32)


def shift(value, axis, step):
    n = lax.axis_size(axis)
    return lax.ppermute(value, axis, [(i, (i + step) % n) for i in range(n)])


def spread(part, width):
    columns = part.shape[1]
    nlat = columns // HEADS
    row = lax.broadcasted_iota(jnp.int32, (HEADS * width, columns), 0) // width
    col = lax.broadcasted_iota(jnp.int32, (HEADS * width, columns), 1) // nlat
    return jnp.where(row == col, jnp.tile(part, (HEADS, 1)), 0.0).astype(BF16)


def by_head(flat, width):
    nlat = flat.shape[1]
    return flat.reshape(HEADS, width, nlat).transpose(1, 0, 2).reshape(width, HEADS * nlat)


def chosen_rows(d):
    v, y, x, c = (lax.axis_index(a) for a in ("v", "y", "x", "c"))
    at = lax.broadcasted_iota(jnp.int32, (32 * CHUNK, 1), 0)
    place, inner = at // CHUNK, at % CHUNK
    dv, i = inner // BLOCK, inner % BLOCK
    dc, dx, dy = place // 16, (place // 4) % 4, place % 4
    owner = ((((v + dv) % 4) * 4 + (y + dy) % 4) * 4 + (x + dx) % 4) * 2 + (c + dc) % 2
    row = jnp.where(inner < 4 * BLOCK, owner * BLOCK + i, -1)
    return (row == lax.broadcasted_iota(jnp.int32, (32 * CHUNK, d), 1)).astype(BF16)


def merge(parts, top_row):
    tops = [p[top_row : top_row + 1] for p in parts]
    top = tops[0]
    for t in tops[1:]:
        top = jnp.maximum(top, t)
    total = sum(p * jnp.exp(t - top) for p, t in zip(parts, tops))
    row = lax.broadcasted_iota(jnp.int32, total.shape, 0)
    return jnp.where(row == top_row, top, total)


def after(value, *others):
    return lax.optimization_barrier((value, *others))[0]


STEP = 512
LONG = 512
GROUP = 4
WINDOW = 384


def group(j, width, nlat):
    start = GROUP * width * j // 128 * 128
    return slice(start, start + WINDOW), slice(GROUP * nlat * j, GROUP * nlat * (j + 1))


def call(body, steps, ins, outs, scratch, flops, moved, name, room):
    def spec(block, where, buffers):
        if block is None:
            return pl.BlockSpec(memory_space=pl.ANY)
        if where is whole_block and buffers:
            return pl.BlockSpec(block, where, pipeline_mode=pl.Buffered(buffers))
        return pl.BlockSpec(block, where)

    return pl.pallas_call(
        body,
        grid=(steps,),
        in_specs=[spec(b, m, 1) for _, b, m in ins],
        out_specs=[spec(b, m, 0) for _, _, b, m in outs],
        out_shape=[jax.ShapeDtypeStruct(s, t) for s, t, _, _ in outs],
        scratch_shapes=scratch,
        compiler_params=pltpu.CompilerParams(vmem_limit_bytes=room * 2**20),
        cost_estimate=pl.CostEstimate(flops=flops, bytes_accessed=moved, transcendentals=0),
        name=name,
    )(*[a for a, _, _ in ins])


def whole_block(i):
    return (0, 0)


def row_block(i):
    return (i, 0)


def col_block(i):
    return (0, i)


def softmax_kernel(
    rows,
    width,
    nlat,
    x_ref,
    gain_ref,
    wk_far,
    wv_far,
    wq_far,
    lat_ref,
    n_ref,
    v_ref,
    e_ref,
    pack_ref,
    sq_far,
    s_all,
    n_all,
    acc_ref,
    state_ref,
    wk_ref,
    wv_ref,
    wq_ref,
    sq_ref,
    wk_sem,
    wv_sem,
    wq_sem,
    sq_sem,
):
    step, steps = pl.program_id(0), pl.num_programs(0) // 2
    at = pl.multiple_of((step % steps) * STEP, STEP)
    here = pl.ds(at, STEP)

    def valid(columns):
        return lax.broadcasted_iota(jnp.int32, (STEP, columns), 0) + at < rows

    wk_copy = pltpu.make_async_copy(wk_far, wk_ref, wk_sem)
    wv_copy = pltpu.make_async_copy(wv_far, wv_ref, wv_sem)
    wq_copy = pltpu.make_async_copy(wq_far, wq_ref, wq_sem)
    sq_copy = pltpu.make_async_copy(sq_ref, sq_far, sq_sem)

    @pl.when(step == 0)
    def _():
        wq_copy.start()
        wk_copy.start()
        wv_copy.start()
        acc_ref[...] = jnp.zeros_like(acc_ref)
        row = lax.broadcasted_iota(jnp.int32, state_ref.shape, 0)
        state_ref[...] = jnp.where(row == 0, -jnp.inf, 0.0)
        wq_copy.wait()
        twice = jnp.concatenate([lat_ref[...], lat_ref[...]], axis=0)
        query = dot(twice, wq_ref[...]).astype(BF16).astype(F32).T
        sq_ref[...] = jnp.zeros_like(sq_ref)
        head_row = lax.broadcasted_iota(jnp.int32, (2 * width, 2 * nlat), 0) // width
        head_col = lax.broadcasted_iota(jnp.int32, (2 * width, 2 * nlat), 1) // nlat
        for t in range(HEADS // 2):
            feat, cols = slice(2 * width * t, 2 * width * (t + 1)), slice(2 * nlat * t, 2 * nlat * (t + 1))
            sq_ref[feat, cols] = jnp.where(head_row == head_col, query[feat, :], 0.0).astype(BF16)
        sq_copy.start()
        wk_copy.wait()

    @pl.when(step < steps)
    def _():
        x = x_ref[...].astype(F32)
        centred = x - jnp.mean(x, axis=-1, keepdims=True)
        rstd = lax.rsqrt(jnp.mean(centred * centred, axis=-1, keepdims=True) + 1e-06)
        normed = centred * rstd * gain_ref[...].astype(F32)[None, :]
        normed = jnp.where(valid(x.shape[1]), normed, 0.0).astype(BF16)
        n_ref[...] = normed
        keys = dot(normed, wk_ref[...]).astype(BF16)
        unused = jnp.where(valid(1), 0.0, -jnp.inf)
        n_all[here, :] = normed
        for j in range(HEADS // GROUP):
            feat, cols = group(j, width, nlat)
            s = dot(keys[:, feat], sq_ref[feat, cols]) * (1.0 / width**0.5) + unused
            s_all[here, cols] = s
            state_ref[0:1, cols] = jnp.maximum(
                state_ref[0:1, cols], jnp.max(s, axis=0, keepdims=True)
            )

    @pl.when(step == steps)
    def _():
        wv_copy.wait()

    @pl.when(step >= steps)
    def _():
        values = dot(n_all[here, :], wv_ref[...]).astype(BF16)
        v_ref[...] = values
        for j in range(HEADS // GROUP):
            feat, cols = group(j, width, nlat)
            e = jnp.exp(s_all[here, cols] - state_ref[0:1, cols])
            state_ref[1:2, cols] += jnp.sum(e, axis=0, keepdims=True)
            e = e.astype(BF16)
            e_ref[:, cols] = e
            acc_ref[j] += dot(values[:, feat], e, 0, 0)

    @pl.when(step == 2 * steps - 1)
    def _():
        for j in range(HEADS // GROUP):
            feat, cols = group(j, width, nlat)
            lane = lax.broadcasted_iota(jnp.int32, (width, GROUP * nlat), 1) // nlat
            out = jnp.zeros((width, GROUP * nlat), F32)
            for g in range(GROUP):
                start = (GROUP * j + g) * width - feat.start
                out = out + jnp.where(lane == g, acc_ref[j, start : start + width, :], 0.0)
            pack_ref[:width, cols] = out
        pack_ref[width:, :] = state_ref[...]
        sq_copy.wait()


def grad_kernel(width, nlat, v_ref, sl_ref, e_ref, state_ref, t_ref, d_ref, keep_ref, send_ref):
    @pl.when(pl.program_id(0) == 0)
    def _():
        keep_ref[...] = jnp.zeros_like(keep_ref)
        send_ref[...] = jnp.zeros_like(send_ref)

    for j in range(HEADS // GROUP):
        feat, cols = group(j, width, nlat)
        dprob = dot(v_ref[:, feat], sl_ref[feat, cols])
        grad = e_ref[:, cols].astype(F32) * (dprob - state_ref[0:1, cols]) * state_ref[1:2, cols]
        d_ref[:, cols] = grad.astype(BF16)
    half = keep_ref.shape[0]
    keep_ref[...] += dot(t_ref[:half, :], d_ref[...])
    send_ref[...] += dot(t_ref[half:, :], d_ref[...])


def back_kernel(d_ref, e_ref, qk_ref, qv_ref, state_ref, x_ref, gain_ref, out_ref, scaled_ref):
    @pl.when(pl.program_id(0) == 0)
    def _():
        scaled_ref[...] = (qv_ref[...].astype(F32) * state_ref[2:3, :]).astype(BF16)

    normed_cot = dot(d_ref[...], qk_ref[...], 1, 1) + dot(e_ref[...], scaled_ref[...], 1, 1)
    x = x_ref[...].astype(F32)
    centred = x - jnp.mean(x, axis=-1, keepdims=True)
    rstd = lax.rsqrt(jnp.mean(centred * centred, axis=-1, keepdims=True) + 1e-06)
    xhat = centred * rstd
    dxhat = normed_cot * gain_ref[...].astype(F32)[None, :]
    mean = jnp.mean(dxhat, axis=-1, keepdims=True)
    slope = jnp.mean(dxhat * xhat, axis=-1, keepdims=True)
    out_ref[...] = ((dxhat - mean - xhat * slope) * rstd).astype(BF16)


def pair_kernel(width, core_ref, own_ref, got_ref, lc_ref, out_ref):
    cut = out_ref.shape[1]
    top = jnp.maximum(own_ref[width : width + 1, :], got_ref[width : width + 1, :])
    here = pl.ds(pl.multiple_of(core_ref[0] * cut, cut), cut)
    own, got = own_ref[:, here], got_ref[:, here]
    own_top, got_top = own[width : width + 1, :], got[width : width + 1, :]
    best = jnp.maximum(own_top, got_top)
    both = own * jnp.exp(own_top - best) + got * jnp.exp(got_top - best)
    row = lax.broadcasted_iota(jnp.int32, both.shape, 0)
    out_ref[: width + 8, :] = jnp.where(row == width, best, both)
    row = lax.broadcasted_iota(jnp.int32, (8, cut), 0)
    out_ref[width + 8 : width + 16, :] = jnp.where(row % 2 == 0, top[:, :cut], top[:, cut:])
    out_ref[width + 16 :, :] = lc_ref[...]


def split_kernel(keep_ref, got_ref, *outs):
    for k in range(4):
        for n in range(4):
            place = slice((4 * k + n) * CHUNK, (4 * k + n + 1) * CHUNK)
            outs[n][k * CHUNK : (k + 1) * CHUNK, :] = keep_ref[place, :] + got_ref[place, :]


def per_device(patches, latents, gain, w_query, w_key, w_value, w_out, cotangent):
    core = lax.axis_index("c")
    frames, latent_rows = patches[0], latents[0]
    rows, d = frames.shape
    nlat = latent_rows.shape[0]
    width = d // HEADS
    scale = 1.0 / width**0.5
    cols = HEADS * nlat
    steps = -(-rows // STEP)
    padded = steps * STEP
    half_rows = 16 * CHUNK

    def own_half(value):
        return lax.dynamic_slice_in_dim(value, core * (cols // 2), cols // 2, 1)

    def whole(half, other):
        return jnp.where(
            core == 0, jnp.concatenate([half, other], 1), jnp.concatenate([other, half], 1)
        )

    lc = by_head(dot(w_out, cotangent[0], 1, 1), width)
    lc = own_half(lc + shift(lc, "c", 1))

    frames_1 = after(frames, lc)
    lc_y = [shift(lc, "y", k) for k in (1, 2, 3)]

    def first(i):
        return (jnp.minimum(i, steps - 1), 0)

    def second(i):
        return (jnp.maximum(i - steps, 0), 0)

    normed, values, expo, pack, spread_q = call(
        functools.partial(softmax_kernel, rows, width, nlat),
        2 * steps,
        [
            (frames_1, (STEP, d), first),
            (gain, (d,), lambda i: (0,)),
            (w_key, None, None),
            (w_value, None, None),
            (w_query, None, None),
            (latent_rows, (nlat, d), whole_block),
        ],
        [
            ((padded, d), BF16, (STEP, d), first),
            ((padded, d), BF16, (STEP, d), second),
            ((padded, cols), BF16, (STEP, cols), second),
            ((width + 8, cols), F32, (width + 8, cols), whole_block),
            ((d, cols), BF16, None, None),
        ],
        [
            pltpu.VMEM((padded, cols), F32),
            pltpu.VMEM((padded, d), BF16),
            pltpu.VMEM((HEADS // GROUP, WINDOW, GROUP * nlat), F32),
            pltpu.VMEM((8, cols), F32),
            pltpu.VMEM((d, d), BF16),
            pltpu.VMEM((d, d), BF16),
            pltpu.VMEM((d, d), BF16),
            pltpu.VMEM((d, cols), BF16),
            pltpu.SemaphoreType.DMA,
            pltpu.SemaphoreType.DMA,
            pltpu.SemaphoreType.DMA,
            pltpu.SemaphoreType.DMA,
        ],
        4 * padded * (d * d + WINDOW * cols),
        6 * padded * d + 2 * padded * cols + 2 * d * (2 * d + cols),
        "softmax",
        56,
    )
    lc = sum(lc_y, after(lc, pack))
    pack = after(pack, lc)
    paired = shift(pack, "c", 1)
    top, top_pair = pack[width : width + 1], paired[width : width + 1]
    top2 = jnp.maximum(top, top_pair)
    vmem = pl.BlockSpec(memory_space=pltpu.VMEM)
    half = pl.pallas_call(
        functools.partial(pair_kernel, width),
        in_specs=[pl.BlockSpec(memory_space=pltpu.SMEM), vmem, vmem, vmem],
        out_specs=vmem,
        out_shape=jax.ShapeDtypeStruct((2 * width + 16, cols // 2), F32),
        compiler_params=pltpu.CompilerParams(vmem_limit_bytes=16 * 2**20),
        name="pair",
    )(core.astype(jnp.int32).reshape(1), pack, paired, lc)

    turned = dot(chosen_rows(d), after(normed, half), 1, 1).astype(BF16)
    halves = [half] + [shift(half, "x", k) for k in (1, 2, 3)]
    tops = [h[width + 8 : width + 10].reshape(1, cols) for h in halves]
    top3 = jnp.maximum(jnp.maximum(tops[0], tops[1]), jnp.maximum(tops[2], tops[3]))
    halves[0] = after(halves[0], turned)
    half = merge([h[: width + 8] for h in halves], width)
    lc = sum(h[width + 16 :] for h in halves)
    lc = whole(lc, shift(lc, "c", 1))
    spread_lc = spread(lc, width)

    half_y = [shift(half, "y", k) for k in (1, 2, 3)]
    u_send = dot(turned[half_rows:], after(expo, half))
    u_got = shift(u_send, "c", 1)
    u = dot(turned[:half_rows], after(expo, u_send))
    half = merge([after(half, u, spread_lc)] + half_y, width)
    pack = whole(half, shift(half, "c", 1))
    gtop, gtotal = pack[width : width + 1], pack[width + 1 : width + 2]
    attn = pack[:width] / gtotal
    factor = jnp.exp(top - gtop) / gtotal
    drift = jnp.sum(lc * attn, axis=0, keepdims=True)
    state = jnp.concatenate([drift, factor * scale, factor, jnp.zeros((5, cols), F32)], axis=0)

    dscore, w, w_send = call(
        functools.partial(grad_kernel, width, nlat),
        padded // LONG,
        [
            (values, (LONG, d), row_block),
            (spread_lc, (d, cols), whole_block),
            (expo, (LONG, cols), row_block),
            (state, (8, cols), whole_block),
            (turned, (2 * half_rows, LONG), col_block),
        ],
        [
            ((padded, cols), BF16, (LONG, cols), row_block),
            ((half_rows, cols), F32, (half_rows, cols), whole_block),
            ((half_rows, cols), F32, (half_rows, cols), whole_block),
        ],
        [],
        2 * padded * cols * (WINDOW + 2 * half_rows),
        2 * padded * (2 * d + 2 * cols) + 12 * half_rows * cols,
        "gradient",
        32,
    )
    w_got = shift(w_send, "c", 1)
    u = after(u, w_send) * jnp.exp(top - top2) + u_got * jnp.exp(top_pair - top2)
    u = u.reshape(4, 4, CHUNK, cols)
    u_x = [shift(u[k], "x", k) for k in (1, 2, 3)]
    cut = jax.ShapeDtypeStruct((4 * CHUNK, cols), F32)
    parts = pl.pallas_call(
        split_kernel,
        out_shape=[cut] * 4,
        compiler_params=pltpu.CompilerParams(vmem_limit_bytes=16 * 2**20),
        cost_estimate=pl.CostEstimate(
            flops=half_rows * cols, bytes_accessed=12 * half_rows * cols, transcendentals=0
        ),
        name="split",
    )(w, w_got)


    q_key = dot(after(w_key, parts[0]), spread_q).astype(BF16)
    q_value = dot(after(w_value, parts[0]), spread_lc).astype(BF16)
    patch_grad = call(
        back_kernel,
        steps,
        [
            (after(dscore, parts[0]), (STEP, cols), row_block),
            (expo, (STEP, cols), row_block),
            (q_key, (d, cols), whole_block),
            (q_value, (d, cols), whole_block),
            (state, (8, cols), whole_block),
            (frames, (STEP, d), row_block),
            (gain, (d,), lambda i: (0,)),
        ],
        [((rows, d), BF16, (STEP, d), row_block)],
        [pltpu.VMEM((d, cols), BF16)],
        4 * padded * d * cols,
        4 * padded * (d + cols) + 4 * d * cols,
        "back",
        28,
    )[0]
    attn_rows = attn.reshape(width, HEADS, nlat).transpose(1, 0, 2).reshape(d, nlat).astype(BF16)
    attended = dot(attn_rows, w_out, 0, 0).astype(BF16)

    u = after(u[0], patch_grad) * jnp.exp(tops[0] - top3) + sum(
        u_x[k - 1] * jnp.exp(tops[k] - top3) for k in (1, 2, 3)
    )
    u = u * (jnp.exp(top3 - gtop) / gtotal)
    w = after(parts[0], patch_grad)
    w = w + shift(parts[1], "y", 1) + shift(parts[2], "y", 2) + shift(parts[3], "y", 3)
    w = w.reshape(4, CHUNK, cols)
    w = w[0] + shift(w[1], "x", 1) + shift(w[2], "x", 2) + shift(w[3], "x", 3)
    u = u[0] + shift(u[1], "y", 1) + shift(u[2], "y", 2) + shift(u[3], "y", 3)
    kv = jnp.concatenate(
        [dot(w.astype(BF16), spread_q, 1, 1), dot(u.astype(BF16), spread_lc, 1, 1)], axis=1
    )
    kv = [kv[k * BLOCK : (k + 1) * BLOCK] for k in range(4)]
    kv_grad = kv[0] + shift(kv[1], "v", 1) + shift(kv[2], "v", 2) + shift(kv[3], "v", 3)
    return (attended[None], patch_grad[None], kv_grad)


def solution(mesh):
    grid = Mesh(mesh.devices.reshape(4, 4, 4, 2), ("v", "y", "x", "c"))
    frame = ("y", "x", "c")
    return jax.shard_map(
        per_device,
        mesh=grid,
        in_specs=(
            P("v", frame, None),
            P("v", None, None),
            P(),
            P(),
            P(),
            P(),
            P(None, frame),
            P("v", None, frame),
        ),
        out_specs=(
            P("v", None, frame),
            P("v", frame, None),
            P(("v", "y", "x", "c"), None),
        ),
        check_vma=False,
    )
```
